256 devices in a mesh: dp: 16 (over x, z_hi, core), sp: 16 (over z_lo, y).
Axes of the slice: x: 4, y: 4, z: 8 (z_hi: 2, z_lo: 4; z = z_hi * 4 + z_lo), core: 2. Of those that a mesh axis runs over, the one named last changes fastest.
Arguments:
- queries: bfloat16 [32768, 4096], P(('dp', 'sp')), may hold values from -5 to 5
- keys: bfloat16 [32768, 1024], P(('dp', 'sp')), may hold values from -5 to 5
- values: bfloat16 [32768, 1024], P(('dp', 'sp')), may hold values from -5 to 5
- out_grad: bfloat16 [32768, 4096], P(('dp', 'sp')), may hold values from -5 to 5
- doc_lengths: int32 [16, 2], replicated, may hold values from 0 to 8, as said below
- owner_docs: int32 [32], replicated, may hold values from 0 to 31, each once
Outputs:
- attn_out: bfloat16 [32768, 4096], P(('dp', 'sp'))
- grad_queries: bfloat16 [32768, 4096], P(('dp', 'sp'))
- grad_keys: bfloat16 [32768, 1024], P(('dp', 'sp'))
- grad_values: bfloat16 [32768, 1024], P(('dp', 'sp'))
The draws below stay inside these ranges and needn't reach their ends.
Inputs may be any that keep to these rules, and one draw needn't show every extreme that they name: `doc_lengths`: row b lists, in units of 256 tokens, the lengths of group b's documents in their order in the group's sequence; each row adds up to 8, every length is a multiple of 4, and zeros stand only after the last document. `owner_docs`: entry p is b * 2 + k for the document k of group b that stands p-th in the owner sequence; every value appears once.
All inputs are finite; a program needn't handle non-finite values.
Results may differ from the reference program's by a relative error of at most 0.0091.
Values may be sent and summed in bfloat16 or wider, within the bound.
No kernel may reach another device: no remote copies, remote signals or barrier semaphores. Data moves between devices by JAX's collectives and lax.ppermute only.
A program may use at most 64 MiB of HBM per device.

```python
import math
import jax
import jax.numpy as jnp
from jax import lax

QH = 32
KVH = 8
HD = 128
TOK_DEV = 128
GROUPS = 16
SPAN = 16
UNIT = 256
GUNITS = 8
STEP = 4
DOCS = 2
GROUP_TOK = 2048
TOKENS = 32768


def draw_queries(key, part):
    key = jax.random.fold_in(key, 4)
    noise_key, scale_key = jax.random.split(key)
    noise_field = jax.random.normal(noise_key, (TOKENS, QH, HD), jnp.float32)
    spread = jnp.exp(jax.random.uniform(scale_key, (TOKENS, QH, 1), jnp.float32, math.log(0.3), math.log(3.0)))
    noise_field = jnp.clip(noise_field * spread, -5.0, 5.0)
    return noise_field.reshape(TOKENS, QH * HD).astype(jnp.bfloat16)


def draw_keys(key, part):
    key = jax.random.fold_in(key, 3)
    noise_key, scale_key = jax.random.split(key)
    noise_field = jax.random.normal(noise_key, (TOKENS, KVH, HD), jnp.float32)
    spread = jnp.exp(jax.random.uniform(scale_key, (TOKENS, KVH, 1), jnp.float32, math.log(0.3), math.log(3.0)))
    noise_field = jnp.clip(noise_field * spread, -5.0, 5.0)
    return noise_field.reshape(TOKENS, KVH * HD).astype(jnp.bfloat16)


def draw_doc_lengths(key, part):
    key = jax.random.fold_in(key, 5)
    cut_key, whole_key = jax.random.split(key)
    cut_flags = jax.random.randint(cut_key, (GROUPS, DOCS - 1), 0, 2, dtype=jnp.int32)
    whole_group = jax.random.randint(whole_key, (), 0, GROUPS, dtype=jnp.int32)
    cut_flags = jnp.where(jnp.arange(GROUPS, dtype=jnp.int32)[:, None] == whole_group, 0, cut_flags)
    start_flags = jnp.concatenate([jnp.ones((GROUPS, 1), jnp.int32), cut_flags], axis=1)
    owner_piece = jnp.cumsum(start_flags, axis=1) - 1
    piece_counts = jnp.sum((owner_piece[:, :, None] == jnp.arange(DOCS, dtype=jnp.int32)[None, None, :]).astype(jnp.int32), axis=1)
    return (piece_counts * STEP).astype(jnp.int32)


def block_scale(own_key, extent, shards, least, top_value):
    loudness = 1.0
    for dim, parts in shards:
        heights = jax.random.uniform(jax.random.fold_in(jax.random.fold_in(own_key, 6), dim), (parts,), jnp.float32, least / len(shards), top_value / len(shards))
        loudness = loudness * jnp.repeat(jnp.exp(heights), extent[dim] // parts).reshape((-1,) + (1,) * (len(extent) - 1 - dim))
    return loudness


def bell_draw(key, dims, scale, bound, shards=(), kind=jnp.bfloat16):
    loudness = block_scale(key, dims, shards, -0.22, 0.18) if shards else 1.0
    entries = jax.random.normal(key, dims, jnp.float32) * scale * loudness
    return jnp.minimum(jnp.maximum(entries, -bound), bound).astype(kind)


def setup_inputs(seed: int = 0) -> dict:
    arg_keys = jax.random.split(jax.random.key(seed), 7)
    return {
        "queries": draw_queries(jax.random.fold_in(arg_keys[6], 71), 0),
        "keys": draw_keys(jax.random.fold_in(arg_keys[6], 71), 0),
        "values": bell_draw(arg_keys[2], (TOKENS, KVH * HD), 1.0, 5.0, ((0, 256),)),
        "out_grad": bell_draw(arg_keys[3], (TOKENS, QH * HD), 1.0, 5.0, ((0, 256),)),
        "doc_lengths": draw_doc_lengths(jax.random.fold_in(arg_keys[6], 71), 0),
        "owner_docs": jax.random.permutation(arg_keys[5], GROUPS * DOCS).astype(jnp.int32),
    }


def unit_sources(doc_lengths, owner_docs):
    lengths = doc_lengths.astype(jnp.int32)
    group_start = (jnp.cumsum(lengths, axis=1) - lengths).astype(jnp.int32)
    ordered = lengths.reshape(-1)[owner_docs]
    ordered_start = (jnp.cumsum(ordered) - ordered).astype(jnp.int32)
    doc_index = jnp.arange(GROUPS * DOCS, dtype=jnp.int32)
    owner_start = lax.optimization_barrier(jnp.sum(jnp.where(owner_docs[None, :] == doc_index[:, None], ordered_start[None, :], 0), axis=1)).astype(jnp.int32).reshape(GROUPS, DOCS)
    slot_index = jnp.arange(GUNITS, dtype=jnp.int32)
    covering = (lax.optimization_barrier(jnp.sum((group_start[:, None, :] <= slot_index[None, :, None]).astype(jnp.int32), axis=2)) - 1).astype(jnp.int32)
    picked = covering[:, :, None] == jnp.arange(DOCS, dtype=jnp.int32)[None, None, :]
    start_group = lax.optimization_barrier(jnp.sum(jnp.where(picked, group_start[:, None, :], 0), axis=2)).astype(jnp.int32)
    start_owner = lax.optimization_barrier(jnp.sum(jnp.where(picked, owner_start[:, None, :], 0), axis=2)).astype(jnp.int32)
    source_unit = (start_owner + slot_index[None, :] - start_group).astype(jnp.int32)
    return (source_unit, covering)

def attend(operands):
    queries_head, keys_head, values_head, grad_head, doc_of_token = operands
    score_scale = 1.0 / math.sqrt(HD)
    position = jnp.arange(GROUP_TOK, dtype=jnp.int32)
    allowed = (doc_of_token[:, None] == doc_of_token[None, :]) & (position[None, :] <= position[:, None])
    scores = jnp.einsum('qhd,kd->hqk', queries_head.astype(jnp.float32), keys_head.astype(jnp.float32)) * score_scale
    scores = jnp.where(allowed[None], scores, -1e+30)
    row_peak = lax.optimization_barrier(jnp.max(scores, axis=-1, keepdims=True))
    weights = jnp.where(allowed[None], jnp.exp(scores - row_peak), 0.0)
    softmax_probs = weights / lax.optimization_barrier(jnp.sum(weights, axis=-1, keepdims=True))
    probs_low = lax.optimization_barrier(softmax_probs.astype(jnp.bfloat16)).astype(jnp.float32)
    attended = jnp.einsum('hqk,kd->qhd', probs_low, values_head.astype(jnp.float32)).astype(jnp.bfloat16)
    attended_wide = lax.optimization_barrier(attended).astype(jnp.float32)
    row_delta = lax.optimization_barrier(jnp.sum(attended_wide * grad_head.astype(jnp.float32), axis=-1))
    dprobs = jnp.einsum('qhd,kd->hqk', grad_head.astype(jnp.float32), values_head.astype(jnp.float32))
    dscores = softmax_probs * (dprobs - row_delta.T[:, :, None])
    dscores_low = lax.optimization_barrier(dscores.astype(jnp.bfloat16)).astype(jnp.float32)
    grad_query = (jnp.einsum('hqk,kd->qhd', dscores_low, keys_head.astype(jnp.float32)) * score_scale).astype(jnp.bfloat16)
    head_keys = (jnp.einsum('hqk,qhd->khd', dscores_low, queries_head.astype(jnp.float32)) * score_scale).astype(jnp.bfloat16)
    head_values = jnp.einsum('hqk,qhd->khd', probs_low, grad_head.astype(jnp.float32)).astype(jnp.bfloat16)
    grad_key = lax.optimization_barrier(jnp.sum(lax.optimization_barrier(head_keys).astype(jnp.float32), axis=1)).astype(jnp.bfloat16)
    grad_value = lax.optimization_barrier(jnp.sum(lax.optimization_barrier(head_values).astype(jnp.float32), axis=1)).astype(jnp.bfloat16)
    return (attended, grad_query, grad_key, grad_value)

def output_rows(tensor):
    features = tensor.shape[2]
    return tensor.reshape(GROUPS, TOK_DEV, SPAN, features).transpose(0, 2, 1, 3).reshape(TOKENS, features)

def reference(queries, keys, values, out_grad, doc_lengths, owner_docs):
    group_ratio = QH // KVH
    source_unit, covering = unit_sources(doc_lengths, owner_docs)
    token_index = jnp.arange(GROUP_TOK, dtype=jnp.int32)
    source_token = (source_unit[:, token_index // UNIT] * UNIT + token_index % UNIT).astype(jnp.int32)
    doc_of_token = covering[:, token_index // UNIT]

    def to_groups(tensor):
        features = tensor.shape[1]
        owner_seq = tensor.reshape(UNIT, TOK_DEV, features).transpose(1, 0, 2).reshape(TOKENS, features)
        return owner_seq[source_token.reshape(-1)].reshape(GROUPS, GROUP_TOK, features)

    def query_heads(tensor):
        return to_groups(tensor).reshape(GROUPS, GROUP_TOK, KVH, group_ratio, HD).transpose(0, 2, 1, 3, 4).reshape(GROUPS * KVH, GROUP_TOK, group_ratio, HD)

    def key_heads(tensor):
        return to_groups(tensor).reshape(GROUPS, GROUP_TOK, KVH, HD).transpose(0, 2, 1, 3).reshape(GROUPS * KVH, GROUP_TOK, HD)
    docs_all = jnp.repeat(doc_of_token, KVH, axis=0)
    attended, grad_query, grad_key, grad_value = lax.map(attend, (query_heads(queries), key_heads(keys), key_heads(values), query_heads(out_grad), docs_all))

    def query_layout(tensor):
        grouped = tensor.reshape(GROUPS, KVH, GROUP_TOK, group_ratio, HD).transpose(0, 2, 1, 3, 4).reshape(GROUPS, GROUP_TOK, QH * HD)
        return output_rows(grouped)

    def key_layout(tensor):
        grouped = tensor.reshape(GROUPS, KVH, GROUP_TOK, HD).transpose(0, 2, 1, 3).reshape(GROUPS, GROUP_TOK, KVH * HD)
        return output_rows(grouped)
    return (query_layout(attended), query_layout(grad_query), key_layout(grad_key), key_layout(grad_value))
```

```python
import math

import jax
import jax.numpy as jnp
from jax import lax
from jax.experimental import pallas as pl
from jax.experimental.pallas import tpu as pltpu
from jax.sharding import PartitionSpec as P

QH = 32
KVH = 8
HD = 128
GROUPS = 16
SPAN = 16
UNITS = 8
UNIT = 256
PACK_STEP = 4
SCALE = 1.0 / math.sqrt(HD)
EXP2_SCALE = SCALE * math.log2(math.e)
NT = (((1,), (1,)), ((), ()))


def dot(left, right):
    return jnp.dot(left, right, preferred_element_type=jnp.float32)


def dot_nt(left, right):
    return lax.dot_general(left, right, NT, preferred_element_type=jnp.float32)


def eye(size):
    row = lax.broadcasted_iota(jnp.int32, (size, size), 0)
    col = lax.broadcasted_iota(jnp.int32, (size, size), 1)
    return jnp.where(row == col, 1.0, 0.0).astype(jnp.bfloat16)


def pack_kernel(len_ref, own_ref, q_ref, k_ref, v_ref, g_ref, out_ref, start_ref, sel_ref):
    @pl.when(pl.program_id(0) == 0)
    def _():
        def place(entry, total):
            doc = own_ref[entry]
            start_ref[doc] = total
            return total + len_ref[doc // 2, doc % 2]

        lax.fori_loop(0, 2 * GROUPS, place, jnp.int32(0))
        unit = lax.broadcasted_iota(jnp.int32, (UNITS, 128), 0)
        column = lax.broadcasted_iota(jnp.int32, (UNITS, 128), 1)
        for b in range(GROUPS):
            first = len_ref[b, 0]
            source = jnp.where(
                unit < first, start_ref[2 * b] + unit, start_ref[2 * b + 1] + unit - first
            )
            sel_ref[b * UNITS : (b + 1) * UNITS, :] = jnp.where(column == source, 1.0, 0.0)

    sel = sel_ref[...].astype(jnp.bfloat16)

    def pick(ref):
        return dot(sel, ref[...]).reshape(GROUPS, UNITS, ref.shape[1])

    q, k, v, g = pick(q_ref), pick(k_ref), pick(v_ref), pick(g_ref)
    for i in range(PACK_STEP):
        heads = slice(i * 2 * HD, (i + 1) * 2 * HD)
        kv = slice((i // 2) * HD, (i // 2 + 1) * HD)
        out_ref[:, i, :, 0 : 2 * HD] = jnp.concatenate(
            [q[:, :, heads], g[:, :, heads]], axis=1
        ).astype(jnp.bfloat16)
        out_ref[:, i, :, 2 * HD :] = jnp.concatenate(
            [k[:, :, kv], v[:, :, kv]], axis=1
        ).astype(jnp.bfloat16)


def pack(doc_lengths, owner_docs, queries, keys, values, out_grad):
    wide = PACK_STEP * 2 * HD
    narrow = PACK_STEP // 2 * HD
    return pl.pallas_call(
        pack_kernel,
        grid=(SPAN // PACK_STEP,),
        in_specs=[
            pl.BlockSpec(memory_space=pltpu.SMEM),
            pl.BlockSpec(memory_space=pltpu.SMEM),
            pl.BlockSpec((128, wide), lambda i: (0, i)),
            pl.BlockSpec((128, narrow), lambda i: (0, i)),
            pl.BlockSpec((128, narrow), lambda i: (0, i)),
            pl.BlockSpec((128, wide), lambda i: (0, i)),
        ],
        out_specs=pl.BlockSpec((GROUPS, PACK_STEP, 16, 3 * HD), lambda i: (0, i, 0, 0)),
        out_shape=jax.ShapeDtypeStruct((GROUPS, SPAN, 16, 3 * HD), jnp.bfloat16),
        scratch_shapes=[
            pltpu.SMEM((2 * GROUPS,), jnp.int32),
            pltpu.VMEM((128, 128), jnp.float32),
        ],
        compiler_params=pltpu.CompilerParams(vmem_limit_bytes=24 * 1024 * 1024),
        name="pack_rows",
    )(doc_lengths, owner_docs, queries, keys, values, out_grad)


def attend_kernel(
    len_ref, x_ref, y_ref, qk_ref, gv_ref, kt_ref, vt_ref, s_ref, bias_ref, dk_ref, dv_ref, ot_ref, dqt_ref
):
    first_len = len_ref[0, 0]
    row = lax.broadcasted_iota(jnp.int32, (256, 256), 0)
    col = lax.broadcasted_iota(jnp.int32, (256, 256), 1)
    wanted = (row % 16) * 16 + (row // 128) * 8 + (row // 16) % 8
    order = jnp.where(col == wanted, 1.0, 0.0).astype(jnp.bfloat16)
    row_pos = (row % 16) * 16 + row // 16
    col_pos = (col % 16) * 16 + col // 16
    bias = jnp.where(row_pos <= col_pos, 0.0, -1e30)
    bias_ref[:, 0:256] = bias
    bias_ref[:, 256:512] = bias

    def sort_slice(s, carry):
        rows = x_ref[:, s].reshape(256, 3 * HD)
        placed = dot(order, rows).astype(jnp.bfloat16).reshape(2, UNITS, 16, 3 * HD)
        here = pl.ds(pl.multiple_of(s * 16, 16), 16)
        qk_ref[:, here, :] = placed[0]
        gv_ref[:, here, :] = placed[1]
        return carry

    lax.fori_loop(0, SPAN, sort_slice, 0)
    eye_hd = eye(HD)

    def turn(c, carry):
        kt_ref[c] = dot_nt(eye_hd, qk_ref[c, :, 2 * HD :]).astype(jnp.bfloat16)
        vt_ref[c] = dot_nt(eye_hd, gv_ref[c, :, 2 * HD :]).astype(jnp.bfloat16)
        dk_ref[c] = jnp.zeros((UNIT, HD), jnp.float32)
        dv_ref[c] = jnp.zeros((UNIT, HD), jnp.float32)
        return carry

    lax.fori_loop(0, UNITS, turn, 0)

    def one_unit(c, carry):
        low = jnp.where(c < first_len, 0, first_len)
        q2 = jnp.concatenate([qk_ref[c, :, 0:HD], qk_ref[c, :, HD : 2 * HD]], axis=0)
        g2 = jnp.concatenate([gv_ref[c, :, 0:HD], gv_ref[c, :, HD : 2 * HD]], axis=0)
        g2t = dot_nt(eye_hd, g2)

        def fold(tile, how):
            return how(tile.reshape(UNIT // 8, 8, 2 * UNIT), axis=0)

        def scores(j, peak):
            tile = dot_nt(qk_ref[j, :, 2 * HD :], q2)
            s_ref[j] = tile
            return jnp.maximum(peak, fold(tile, jnp.max))

        own = dot_nt(qk_ref[c, :, 2 * HD :], q2) + bias_ref[...]
        s_ref[c] = own
        peak = lax.fori_loop(low, c, scores, fold(own, jnp.max))
        peak = jnp.max(peak, axis=0, keepdims=True) * EXP2_SCALE

        def weights(j, norm):
            tile = jnp.exp2(s_ref[j] * EXP2_SCALE - peak)
            s_ref[j] = tile
            return norm + fold(tile, jnp.sum)

        norm = lax.fori_loop(low, c + 1, weights, jnp.zeros((8, 2 * UNIT), jnp.float32))
        inverse = 1.0 / jnp.sum(norm, axis=0, keepdims=True)
        ot_ref[...] = jnp.zeros_like(ot_ref)
        dqt_ref[...] = jnp.zeros_like(dqt_ref)

        def forward(j, carry):
            probs = s_ref[j] * inverse
            s_ref[j] = probs
            probs_low = probs.astype(jnp.bfloat16)
            dv_ref[j] += dot(probs_low, g2)
            ot_ref[...] += dot(vt_ref[j], probs_low)
            return carry

        lax.fori_loop(low, c + 1, forward, 0)
        out_low = ot_ref[...].astype(jnp.bfloat16)
        delta = jnp.sum(out_low.astype(jnp.float32) * g2t, axis=0, keepdims=True)

        def backward(j, carry):
            dprobs = dot_nt(gv_ref[j, :, 2 * HD :], g2)
            dscores = (s_ref[j] * (dprobs - delta)).astype(jnp.bfloat16)
            dk_ref[j] += dot(dscores, q2)
            dqt_ref[...] += dot(kt_ref[j], dscores)
            return carry

        lax.fori_loop(low, c + 1, backward, 0)
        dq_low = (dqt_ref[...] * SCALE).astype(jnp.bfloat16)
        rows = pl.ds(pl.multiple_of(c * 16, 16), 16)
        eye_unit = eye(UNIT)
        for h in range(2):
            part = slice(h * UNIT, (h + 1) * UNIT)
            out_rows = dot_nt(eye_unit, out_low[:, part]).astype(jnp.bfloat16)
            dq_rows = dot_nt(eye_unit, dq_low[:, part]).astype(jnp.bfloat16)
            y_ref[:, rows, h * HD : (h + 1) * HD] = out_rows.reshape(SPAN, 16, HD)
            y_ref[:, rows, (2 + h) * HD : (3 + h) * HD] = dq_rows.reshape(SPAN, 16, HD)
        return carry

    lax.fori_loop(0, UNITS, one_unit, 0)

    def finish(c, carry):
        rows = pl.ds(pl.multiple_of(c * 16, 16), 16)
        dk = (dk_ref[c] * SCALE).astype(jnp.bfloat16)
        dv = dv_ref[c].astype(jnp.bfloat16)
        y_ref[:, rows, 4 * HD : 5 * HD] = dk.reshape(SPAN, 16, HD)
        y_ref[:, rows, 5 * HD : 6 * HD] = dv.reshape(SPAN, 16, HD)
        return carry

    lax.fori_loop(0, UNITS, finish, 0)


def attend(lengths, x):
    return pl.pallas_call(
        attend_kernel,
        in_specs=[
            pl.BlockSpec(memory_space=pltpu.SMEM),
            pl.BlockSpec(memory_space=pltpu.VMEM),
        ],
        out_specs=pl.BlockSpec(memory_space=pltpu.VMEM),
        out_shape=jax.ShapeDtypeStruct((SPAN, 128, 6 * HD), jnp.bfloat16),
        scratch_shapes=[
            pltpu.VMEM((UNITS, UNIT, 3 * HD), jnp.bfloat16),
            pltpu.VMEM((UNITS, UNIT, 3 * HD), jnp.bfloat16),
            pltpu.VMEM((UNITS, HD, UNIT), jnp.bfloat16),
            pltpu.VMEM((UNITS, HD, UNIT), jnp.bfloat16),
            pltpu.VMEM((UNITS, UNIT, 2 * UNIT), jnp.float32),
            pltpu.VMEM((UNIT, 2 * UNIT), jnp.float32),
            pltpu.VMEM((UNITS, UNIT, HD), jnp.float32),
            pltpu.VMEM((UNITS, UNIT, HD), jnp.float32),
            pltpu.VMEM((HD, 2 * UNIT), jnp.float32),
            pltpu.VMEM((HD, 2 * UNIT), jnp.float32),
        ],
        compiler_params=pltpu.CompilerParams(vmem_limit_bytes=40 * 1024 * 1024),
        name="attend",
    )(lengths, x)


def unpack_kernel(z_ref, out_ref, dq_ref, dk_ref, dv_ref):
    for i in range(PACK_STEP):
        out_ref[:, i * 2 * HD : (i + 1) * 2 * HD] = z_ref[i, :, 0 : 2 * HD]
        dq_ref[:, i * 2 * HD : (i + 1) * 2 * HD] = z_ref[i, :, 2 * HD : 4 * HD]
    for i in range(PACK_STEP // 2):
        pair = z_ref[2 * i, :, 4 * HD :].astype(jnp.float32) + z_ref[2 * i + 1, :, 4 * HD :].astype(
            jnp.float32
        )
        dk_ref[:, i * HD : (i + 1) * HD] = pair[:, :HD].astype(jnp.bfloat16)
        dv_ref[:, i * HD : (i + 1) * HD] = pair[:, HD:].astype(jnp.bfloat16)


def unpack(z):
    wide = PACK_STEP * 2 * HD
    narrow = PACK_STEP // 2 * HD
    return pl.pallas_call(
        unpack_kernel,
        grid=(SPAN // PACK_STEP,),
        in_specs=[pl.BlockSpec((PACK_STEP, 128, 6 * HD), lambda i: (i, 0, 0))],
        out_specs=[
            pl.BlockSpec((128, wide), lambda i: (0, i)),
            pl.BlockSpec((128, wide), lambda i: (0, i)),
            pl.BlockSpec((128, narrow), lambda i: (0, i)),
            pl.BlockSpec((128, narrow), lambda i: (0, i)),
        ],
        out_shape=[
            jax.ShapeDtypeStruct((128, QH * HD), jnp.bfloat16),
            jax.ShapeDtypeStruct((128, QH * HD), jnp.bfloat16),
            jax.ShapeDtypeStruct((128, KVH * HD), jnp.bfloat16),
            jax.ShapeDtypeStruct((128, KVH * HD), jnp.bfloat16),
        ],
        compiler_params=pltpu.CompilerParams(vmem_limit_bytes=24 * 1024 * 1024),
        name="unpack_heads",
    )(z)


def body(queries, keys, values, out_grad, doc_lengths, owner_docs):
    lengths = lax.dynamic_slice_in_dim(doc_lengths, lax.axis_index("dp"), 1, 0)
    packed = pack(doc_lengths, owner_docs, queries, keys, values, out_grad)
    arrived = lax.all_to_all(
        packed.reshape(GROUPS * SPAN, 16, 3 * HD), ("dp", "sp"), split_axis=0, concat_axis=0, tiled=True
    )
    done = attend(lengths, arrived.reshape(GROUPS, SPAN, 16, 3 * HD))
    returned = lax.all_to_all(done, "sp", split_axis=0, concat_axis=0, tiled=True)
    return tuple(unpack(returned))


def solution(mesh):
    rows = P(("dp", "sp"), None)
    return jax.shard_map(
        body,
        mesh=mesh,
        in_specs=(rows, rows, rows, rows, P(), P()),
        out_specs=(rows, rows, rows, rows),
        check_vma=False,
    )
```

```python
import functools
import math

import jax
import jax.numpy as jnp
from jax import lax
from jax.experimental import pallas as pl
from jax.experimental.pallas import tpu as pltpu
from jax.sharding import Mesh
from jax.sharding import PartitionSpec as P

QH = 32
KVH = 8
HD = 128
GROUPS = 16
UNITS = 8
BLOCKS = 8
SPAN = 16
RATIO = QH // KVH
QROWS = RATIO * 128
LANES = RATIO * HD + HD
PACK_STEP = 2
SCALE = 1.0 / math.sqrt(HD)
EXP2_SCALE = SCALE * math.log2(math.e)
NT = (((1,), (1,)), ((), ()))
MIB = 1024 * 1024
SMEM = pl.BlockSpec(memory_space=pltpu.SMEM)
VMEM = pl.BlockSpec(memory_space=pltpu.VMEM)


def shape(dims, kind=jnp.bfloat16):
    return jax.ShapeDtypeStruct(dims, kind)


def dot(left, right):
    return jnp.dot(left, right, preferred_element_type=jnp.float32)


def dot_nt(left, right):
    return lax.dot_general(left, right, NT, preferred_element_type=jnp.float32)


def low(value):
    return value.astype(jnp.bfloat16)


def eye(size):
    row = lax.broadcasted_iota(jnp.int32, (size, size), 0)
    col = lax.broadcasted_iota(jnp.int32, (size, size), 1)
    return low(jnp.where(row == col, 1.0, 0.0))


def take_order():
    row = lax.broadcasted_iota(jnp.int32, (256, 256), 0)
    col = lax.broadcasted_iota(jnp.int32, (256, 256), 1)
    wanted = (row % 8) * 32 + (row // 8 % 2) * 16 + (row // 128) * 8 + (row // 16) % 8
    return low(jnp.where(col == wanted, 1.0, 0.0))


def pack_kernel(len_ref, own_ref, q_ref, k_ref, v_ref, g_ref, out_ref, start_ref, sel_ref):
    @pl.when(pl.program_id(0) == 0)
    def _():
        def place(entry, total):
            doc = own_ref[entry]
            start_ref[doc] = total
            return total + len_ref[doc // 2, doc % 2]

        lax.fori_loop(0, 2 * GROUPS, place, jnp.int32(0))
        unit = lax.broadcasted_iota(jnp.int32, (UNITS, 128), 0)
        column = lax.broadcasted_iota(jnp.int32, (UNITS, 128), 1)
        for b in range(GROUPS):
            first = len_ref[b, 0]
            source = jnp.where(
                unit < first, start_ref[2 * b] + unit, start_ref[2 * b + 1] + unit - first
            )
            sel_ref[b * UNITS : (b + 1) * UNITS, :] = jnp.where(column == source, 1.0, 0.0)

    sel = low(sel_ref[...])

    def pick(ref):
        return dot(sel, ref[...]).reshape(GROUPS, UNITS, ref.shape[1])

    q, k, v, g = pick(q_ref), pick(k_ref), pick(v_ref), pick(g_ref)
    for i in range(PACK_STEP):
        heads = slice(i * RATIO * HD, (i + 1) * RATIO * HD)
        kv = slice(i * HD, (i + 1) * HD)
        wide = low(jnp.concatenate([q[:, :, heads], g[:, :, heads]], axis=1))
        narrow = low(jnp.concatenate([k[:, :, kv], v[:, :, kv]], axis=1))
        out_ref[:, i, :, :, 0 : RATIO * HD] = wide.reshape(BLOCKS, 2, 16, RATIO * HD)
        out_ref[:, i, :, :, RATIO * HD :] = narrow.reshape(BLOCKS, 2, 16, HD)


def pack(doc_lengths, owner_docs, queries, keys, values, out_grad):
    wide = PACK_STEP * RATIO * HD
    narrow = PACK_STEP * HD
    return pl.pallas_call(
        pack_kernel,
        grid=(KVH // PACK_STEP,),
        in_specs=[
            SMEM,
            SMEM,
            pl.BlockSpec((128, wide), lambda i: (0, i)),
            pl.BlockSpec((128, narrow), lambda i: (0, i)),
            pl.BlockSpec((128, narrow), lambda i: (0, i)),
            pl.BlockSpec((128, wide), lambda i: (0, i)),
        ],
        out_specs=pl.BlockSpec((BLOCKS, PACK_STEP, 2, 16, LANES), lambda i: (0, i, 0, 0, 0)),
        out_shape=shape((BLOCKS, KVH, 2, 16, LANES)),
        scratch_shapes=[pltpu.SMEM((2 * GROUPS,), jnp.int32), pltpu.VMEM((128, 128), jnp.float32)],
        compiler_params=pltpu.CompilerParams(vmem_limit_bytes=56 * MIB),
        name="pack_rows",
    )(doc_lengths, owner_docs, queries, keys, values, out_grad)


def fold(tile, how):
    return how(tile.reshape(tile.shape[0] // 8, 8, tile.shape[1]), axis=0)


def causal_bias(core):
    key = lax.broadcasted_iota(jnp.int32, (256, QROWS), 0)
    query = lax.broadcasted_iota(jnp.int32, (256, QROWS), 1)
    key_core = jnp.where(key < 128, core, 1 - core)
    key_pos = (key % 8) * 32 + key_core * 16 + (key // 8) % SPAN
    query_pos = (query % 8) * 32 + core * 16 + (query // 8) % SPAN
    return jnp.where(key_pos <= query_pos, 0.0, -1e30)


def sort_rows(order, ref, part, lanes):
    rows = ref[:, 2 * part : 2 * part + 2, :, lanes]
    return low(dot(order, rows.reshape(256, rows.shape[3])))


def place_heads(placed, part, ref):
    for h in range(RATIO):
        ref[:, h * 128 + part * 16 : h * 128 + (part + 1) * 16, :] = placed[
            :, h * HD : (h + 1) * HD
        ].reshape(UNITS, 16, HD)


def unit_rows(c):
    return pl.ds(pl.multiple_of(c * 8, 8), 8)


def forward_kernel(
    info_ref, x_ref, oth_ref, o_ref, q_ref, k_ref, v_ref, stat_ref, vt_ref, s_ref, bias_ref, ot_ref, wide_ref
):
    core, first_len = info_ref[0], info_ref[1]
    order = take_order()
    bias_ref[...] = causal_bias(core)
    for part in range(SPAN // 2):
        for base, placed in (
            (0, sort_rows(order, x_ref, part, slice(RATIO * HD, LANES))),
            (128, sort_rows(order, oth_ref, part, slice(0, HD))),
        ):
            here = slice(base + part * 16, base + (part + 1) * 16)
            k_ref[:, here, :] = placed[:128].reshape(UNITS, 16, HD)
            v_ref[:, here, :] = placed[128:].reshape(UNITS, 16, HD)
        place_heads(sort_rows(order[:128], x_ref, part, slice(0, RATIO * HD)), part, q_ref)
    eye_hd = eye(HD)
    for c in range(UNITS):
        vt_ref[c] = low(dot_nt(eye_hd, v_ref[c]))

    def one_unit(c, carry):
        begin = jnp.where(c < first_len, 0, first_len)
        q4 = q_ref[c]

        def scores(j, peak):
            tile = dot_nt(k_ref[j], q4)
            s_ref[j] = tile
            return jnp.maximum(peak, fold(tile, jnp.max))

        own = dot_nt(k_ref[c], q4) + bias_ref[...]
        s_ref[c] = own
        peak = lax.fori_loop(begin, c, scores, fold(own, jnp.max))
        peak = jnp.max(peak, axis=0, keepdims=True) * EXP2_SCALE

        def weights(j, norm):
            tile = jnp.exp2(s_ref[j] * EXP2_SCALE - peak)
            s_ref[j] = tile
            return norm + fold(tile, jnp.sum)

        norm = lax.fori_loop(begin, c + 1, weights, jnp.zeros((8, QROWS), jnp.float32))
        inverse = 1.0 / jnp.sum(norm, axis=0, keepdims=True)
        stat_ref[c, 0:1, :] = peak
        stat_ref[c, 1:2, :] = inverse
        ot_ref[...] = jnp.zeros_like(ot_ref)

        def attended(j, carry):
            ot_ref[...] += dot(vt_ref[j], low(s_ref[j] * inverse))
            return carry

        lax.fori_loop(begin, c + 1, attended, 0)
        out_low = low(ot_ref[...])
        for h in range(RATIO):
            part = dot_nt(eye_hd, out_low[:, h * 128 : (h + 1) * 128])
            wide_ref[:, unit_rows(c), h * HD : (h + 1) * HD] = part.reshape(SPAN, 8, HD)
        return carry

    lax.fori_loop(0, UNITS, one_unit, 0)
    o_ref[...] = low(wide_ref[...])


def forward(info, arrived, kv_oth):
    return pl.pallas_call(
        forward_kernel,
        in_specs=[SMEM, VMEM, VMEM],
        out_specs=[VMEM] * 5,
        out_shape=[
            shape((SPAN, 64, RATIO * HD)),
            shape((UNITS, QROWS, HD)),
            shape((UNITS, 256, HD)),
            shape((UNITS, 256, HD)),
            shape((UNITS, 8, QROWS), jnp.float32),
        ],
        scratch_shapes=[
            pltpu.VMEM((UNITS, HD, 256), jnp.bfloat16),
            pltpu.VMEM((UNITS, 256, QROWS), jnp.float32),
            pltpu.VMEM((256, QROWS), jnp.float32),
            pltpu.VMEM((HD, QROWS), jnp.float32),
            pltpu.VMEM((SPAN, 64, RATIO * HD), jnp.float32),
        ],
        compiler_params=pltpu.CompilerParams(vmem_limit_bytes=40 * MIB),
        cost_estimate=pl.CostEstimate(
            flops=5_000_000_000, bytes_accessed=8_000_000, transcendentals=5_000_000
        ),
        name="attend_forward",
    )(info, arrived, kv_oth)


def backward_kernel(
    info_ref, x_ref, q_ref, k_ref, v_ref, o_ref, stat_ref, dq_ref, own_ref, oth_ref, g_ref, kt_ref, bias_ref, dk_ref, dv_ref, dqt_ref, wide_ref, owide_ref
):
    core, first_len = info_ref[0], info_ref[1]
    order = take_order()
    bias_ref[...] = causal_bias(core)
    owide_ref[...] = o_ref[...].astype(jnp.float32)
    for part in range(SPAN // 2):
        place_heads(sort_rows(order[128:], x_ref, part, slice(0, RATIO * HD)), part, g_ref)
    eye_hd = eye(HD)
    for c in range(UNITS):
        kt_ref[c] = low(dot_nt(eye_hd, k_ref[c]))
    dk_ref[...] = jnp.zeros_like(dk_ref)
    dv_ref[...] = jnp.zeros_like(dv_ref)

    def one_unit(c, carry):
        begin = jnp.where(c < first_len, 0, first_len)
        q4, g4 = q_ref[c], g_ref[c]
        out = low(owide_ref[:, unit_rows(c), :].reshape(128, RATIO * HD))
        delta = jnp.concatenate(
            [
                jnp.sum(
                    dot_nt(eye_hd, out[:, h * HD : (h + 1) * HD])
                    * dot_nt(eye_hd, g4[h * 128 : (h + 1) * 128]),
                    axis=0,
                    keepdims=True,
                )
                for h in range(RATIO)
            ],
            axis=1,
        )
        peak, inverse = stat_ref[c, 0:1, :], stat_ref[c, 1:2, :]
        dqt_ref[...] = jnp.zeros_like(dqt_ref)

        def tile(j, tile_scores):
            probs = jnp.exp2(tile_scores * EXP2_SCALE - peak) * inverse
            dv_ref[j] += dot(low(probs), g4)
            dscores = low(probs * (dot_nt(v_ref[j], g4) - delta))
            dk_ref[j] += dot(dscores, q4)
            dqt_ref[...] += dot(kt_ref[j], dscores)

        def full(j, carry):
            tile(j, dot_nt(k_ref[j], q4))
            return carry

        lax.fori_loop(begin, c, full, 0)
        tile(c, dot_nt(k_ref[c], q4) + bias_ref[...])
        dq_low = low(dqt_ref[...] * SCALE)
        for h in range(RATIO):
            part = dot_nt(eye_hd, dq_low[:, h * 128 : (h + 1) * 128])
            wide_ref[:, unit_rows(c), h * HD : (h + 1) * HD] = part.reshape(SPAN, 8, HD)
        return carry

    lax.fori_loop(0, UNITS, one_unit, 0)
    dq_ref[...] = low(wide_ref[...])
    for c in range(UNITS):
        rows = slice(c * 8, (c + 1) * 8)
        own_ref[:, rows, 0:HD] = (dk_ref[c, 0:128] * SCALE).reshape(SPAN, 8, HD)
        own_ref[:, rows, HD:] = dv_ref[c, 0:128].reshape(SPAN, 8, HD)
        wide_ref[:, rows, 0:HD] = (dk_ref[c, 128:] * SCALE).reshape(SPAN, 8, HD)
        wide_ref[:, rows, HD : 2 * HD] = dv_ref[c, 128:].reshape(SPAN, 8, HD)
    oth_ref[...] = low(wide_ref[:, :, 0 : 2 * HD])


def backward(info, qg, q, k, v, out, stats):
    return pl.pallas_call(
        backward_kernel,
        in_specs=[SMEM] + [VMEM] * 6,
        out_specs=[VMEM] * 3,
        out_shape=[
            shape((SPAN, 64, RATIO * HD)),
            shape((SPAN, 64, 2 * HD), jnp.float32),
            shape((SPAN, 64, 2 * HD)),
        ],
        scratch_shapes=[
            pltpu.VMEM((UNITS, QROWS, HD), jnp.bfloat16),
            pltpu.VMEM((UNITS, HD, 256), jnp.bfloat16),
            pltpu.VMEM((256, QROWS), jnp.float32),
            pltpu.VMEM((UNITS, 256, HD), jnp.float32),
            pltpu.VMEM((UNITS, 256, HD), jnp.float32),
            pltpu.VMEM((HD, QROWS), jnp.float32),
            pltpu.VMEM((SPAN, 64, RATIO * HD), jnp.float32),
            pltpu.VMEM((SPAN, 64, RATIO * HD), jnp.float32),
        ],
        compiler_params=pltpu.CompilerParams(vmem_limit_bytes=40 * MIB),
        cost_estimate=pl.CostEstimate(
            flops=12_000_000_000, bytes_accessed=8_000_000, transcendentals=5_000_000
        ),
        name="attend_backward",
    )(info, qg, q, k, v, out, stats)


def join_kernel(dq_ref, own_ref, oth_ref, out_ref):
    out_ref[:, :, 0 : RATIO * HD] = dq_ref[...]
    out_ref[:, :, RATIO * HD :] = low(own_ref[...] + oth_ref[...].astype(jnp.float32))


def join(dq, own, oth):
    return pl.pallas_call(
        join_kernel,
        in_specs=[VMEM] * 3,
        out_specs=VMEM,
        out_shape=shape((SPAN, 64, 6 * HD)),
        compiler_params=pltpu.CompilerParams(vmem_limit_bytes=24 * MIB),
        name="join_gradients",
    )(dq, own, oth)


def row_order(core):
    row = lax.broadcasted_iota(jnp.int32, (128, 128), 0)
    col = lax.broadcasted_iota(jnp.int32, (128, 128), 1)
    other = jnp.where(row % 2 == core, 0, 64)
    return low(jnp.where(col == other + (row // 16) * 8 + (row % 16) // 2, 1.0, 0.0))


def unpack_kernel(widths, info_ref, z_ref, oth_ref, *out_refs):
    core = info_ref[0]
    order = row_order(core)
    for g in range(KVH):
        both = jnp.concatenate([z_ref[g, core], oth_ref[g]], axis=0)
        placed = low(dot(order, both))
        begin = 0
        for width, ref in zip(widths, out_refs):
            ref[:, g * width : (g + 1) * width] = placed[:, begin : begin + width]
            begin += width


def unpack(info, z, oth, widths):
    return pl.pallas_call(
        functools.partial(unpack_kernel, widths),
        in_specs=[SMEM, VMEM, VMEM],
        out_specs=[VMEM] * len(widths),
        out_shape=[shape((128, KVH * width)) for width in widths],
        compiler_params=pltpu.CompilerParams(vmem_limit_bytes=24 * MIB),
        name="unpack_rows",
    )(info, z, oth)


def body(queries, keys, values, out_grad, doc_lengths, owner_docs):
    core = lax.axis_index("core")
    group = lax.axis_index("block") * 2 + lax.axis_index("sp") % 2
    first = lax.dynamic_slice(doc_lengths, (group, 0), (1, 1)).reshape(1)
    info = jnp.concatenate([core.reshape(1), first])

    def swap(tensor):
        return lax.ppermute(tensor, "core", [(0, 1), (1, 0)])

    def spread(tensor):
        return lax.all_to_all(tensor, "sp", split_axis=0, concat_axis=0, tiled=True)

    def finish(tensor, widths):
        split = tensor.reshape((KVH, 2) + tensor.shape[1:])
        oth = swap(lax.dynamic_index_in_dim(split, 1 - core, 1, keepdims=False))
        return unpack(info, split, oth, widths)

    packed = pack(doc_lengths, owner_docs, queries, keys, values, out_grad)
    arrived = lax.all_to_all(
        packed.reshape(BLOCKS * SPAN, 16, LANES), ("block", "sp"), split_axis=0, concat_axis=0, tiled=True
    ).reshape(BLOCKS, SPAN, 16, LANES)
    kv_oth = swap(arrived[:, :, :, RATIO * HD :])
    out, q, k, v, stats = forward(info, arrived, kv_oth)
    out_back = spread(out)
    dq, own, oth = backward(info, arrived, q, k, v, out, stats)
    back = spread(join(dq, own, swap(oth)))
    (attn_out,) = finish(out_back, (RATIO * HD,))
    return (attn_out, *finish(back, (RATIO * HD, HD, HD)))


def solution(mesh):
    cut = Mesh(mesh.devices.reshape(BLOCKS, 2, SPAN), ("block", "core", "sp"))
    rows = P(("block", "core", "sp"), None)
    return jax.shard_map(
        body,
        mesh=cut,
        in_specs=(rows, rows, rows, rows, P(), P()),
        out_specs=(rows, rows, rows, rows),
        check_vma=False,
    )
```

```python
import functools
import math

import jax
import jax.numpy as jnp
from jax import lax
from jax.experimental import pallas as pl
from jax.experimental.pallas import tpu as pltpu
from jax.sharding import Mesh
from jax.sharding import PartitionSpec as P

QH = 32
KVH = 8
HD = 128
GROUPS = 16
UNITS = 8
BLOCKS = 8
SPAN = 16
RATIO = QH // KVH
QROWS = RATIO * 128
PAIR = 2 * HD
LANES = PAIR + HD
PACK_STEP = 2
SCALE = 1.0 / math.sqrt(HD)
EXP2_SCALE = SCALE * math.log2(math.e)
NT = (((1,), (1,)), ((), ()))
MIB = 1024 * 1024
SMEM = pl.BlockSpec(memory_space=pltpu.SMEM)
VMEM = pl.BlockSpec(memory_space=pltpu.VMEM)


def shape(dims, kind=jnp.bfloat16):
    return jax.ShapeDtypeStruct(dims, kind)


def dot(left, right):
    return jnp.dot(left, right, preferred_element_type=jnp.float32)


def dot_nt(left, right):
    return lax.dot_general(left, right, NT, preferred_element_type=jnp.float32)


def low(value):
    return value.astype(jnp.bfloat16)


def eye(size):
    row = lax.broadcasted_iota(jnp.int32, (size, size), 0)
    col = lax.broadcasted_iota(jnp.int32, (size, size), 1)
    return low(jnp.where(row == col, 1.0, 0.0))


def take_order():
    row = lax.broadcasted_iota(jnp.int32, (256, 256), 0)
    col = lax.broadcasted_iota(jnp.int32, (256, 256), 1)
    wanted = (row % 8) * 32 + (row // 8 % 2) * 16 + (row // 128) * 8 + (row // 16) % 8
    return low(jnp.where(col == wanted, 1.0, 0.0))


def select_rows(len_ref, own_ref, start_ref, sel_ref):
    def place(entry, total):
        doc = own_ref[entry]
        start_ref[doc] = total
        return total + len_ref[doc % 2, doc // 2]

    lax.fori_loop(0, 2 * GROUPS, place, jnp.int32(0))
    unit = lax.broadcasted_iota(jnp.int32, (UNITS, 128), 0)
    column = lax.broadcasted_iota(jnp.int32, (UNITS, 128), 1)
    for b in range(GROUPS):
        first = len_ref[0, b]
        source = jnp.where(
            unit < first, start_ref[2 * b] + unit, start_ref[2 * b + 1] + unit - first
        )
        sel_ref[b * UNITS : (b + 1) * UNITS, :] = jnp.where(column == source, 1.0, 0.0)


def pack_kernel(len_ref, own_ref, wide_ref, *refs):
    (*narrow_refs, out_ref, start_ref, sel_ref) = refs

    @pl.when(pl.program_id(0) == 0)
    def _():
        select_rows(len_ref, own_ref, start_ref, sel_ref)

    sel = low(sel_ref[...])

    def pick(ref):
        return dot(sel, ref[...]).reshape(GROUPS, UNITS, ref.shape[1])

    wide = pick(wide_ref)
    narrow = [pick(ref) for ref in narrow_refs]
    for i in range(PACK_STEP):
        begin = i * RATIO * HD
        first, second = wide[:, :, begin : begin + PAIR], wide[:, :, begin + PAIR : begin + 2 * PAIR]
        both = low(jnp.concatenate([first, second], axis=1))
        out_ref[:, i, :, :, 0:PAIR] = both.reshape(BLOCKS, 2, 16, PAIR)
        if narrow:
            both = low(jnp.concatenate([n[:, :, i * HD : (i + 1) * HD] for n in narrow], axis=1))
            out_ref[:, i, :, :, PAIR:] = both.reshape(BLOCKS, 2, 16, HD)


def pack(name, lengths, owner_docs, wide, *narrow):
    lanes = PAIR + (HD if narrow else 0)
    return pl.pallas_call(
        pack_kernel,
        grid=(KVH // PACK_STEP,),
        in_specs=[SMEM, SMEM, pl.BlockSpec((128, PACK_STEP * RATIO * HD), lambda i: (0, i))]
        + [pl.BlockSpec((128, PACK_STEP * HD), lambda i: (0, i)) for _ in narrow],
        out_specs=pl.BlockSpec((BLOCKS, PACK_STEP, 2, 16, lanes), lambda i: (0, i, 0, 0, 0)),
        out_shape=shape((BLOCKS, KVH, 2, 16, lanes)),
        scratch_shapes=[pltpu.SMEM((2 * GROUPS,), jnp.int32), pltpu.VMEM((128, 128), jnp.float32)],
        compiler_params=pltpu.CompilerParams(vmem_limit_bytes=56 * MIB),
        name=name,
    )(lengths, owner_docs, wide, *narrow)


def fold(tile, how):
    return how(tile.reshape(tile.shape[0] // 8, 8, tile.shape[1]), axis=0)


def place(len_ref):
    group = lax.axis_index("block") * 2 + lax.axis_index("sp") % 2
    return lax.axis_index("core"), len_ref[0, group]


def causal_bias(core):
    key = lax.broadcasted_iota(jnp.int32, (256, QROWS), 0)
    query = lax.broadcasted_iota(jnp.int32, (256, QROWS), 1)
    key_core = jnp.where(key < 128, core, 1 - core)
    key_pos = (key % 8) * 32 + key_core * 16 + (key // 8) % SPAN
    query_pos = (query % 8) * 32 + core * 16 + (query // 8) % SPAN
    return jnp.where(key_pos <= query_pos, 0.0, -1e30)


def sort_rows(order, ref, part):
    rows = ref[:, 2 * part : 2 * part + 2]
    return low(dot(order, rows.reshape(256, rows.shape[3])))


def place_heads(placed, part, ref):
    for h in range(RATIO):
        here = slice(h * 128 + part * 16, h * 128 + (part + 1) * 16)
        row, lane = (h // 2) * 128, (h % 2) * HD
        ref[:, here, :] = placed[row : row + 128, lane : lane + HD].reshape(UNITS, 16, HD)


def unit_rows(c):
    return pl.ds(pl.multiple_of(c * 8, 8), 8)


def forward_kernel(
    info_ref, x_ref, oth_ref, o_ref, q_ref, k_ref, v_ref, stat_ref, vt_ref, s_ref, bias_ref, ot_ref, wide_ref
):
    core, first_len = place(info_ref)
    order = take_order()
    bias_ref[...] = causal_bias(core)
    for part in range(SPAN // 2):
        own = sort_rows(order, x_ref, part)
        place_heads(own, part, q_ref)
        for base, placed in ((0, own[:, PAIR:]), (128, sort_rows(order, oth_ref, part))):
            here = slice(base + part * 16, base + (part + 1) * 16)
            k_ref[:, here, :] = placed[:128].reshape(UNITS, 16, HD)
            v_ref[:, here, :] = placed[128:].reshape(UNITS, 16, HD)
    eye_hd = eye(HD)
    for c in range(UNITS):
        vt_ref[c] = low(dot_nt(eye_hd, v_ref[c]))

    def one_unit(c, carry):
        begin = jnp.where(c < first_len, 0, first_len)
        q4 = q_ref[c]

        def scores(j, peak):
            tile = dot_nt(k_ref[j], q4)
            s_ref[j] = tile
            return jnp.maximum(peak, fold(tile, jnp.max))

        own = dot_nt(k_ref[c], q4) + bias_ref[...]
        s_ref[c] = own
        peak = lax.fori_loop(begin, c, scores, fold(own, jnp.max))
        peak = jnp.max(peak, axis=0, keepdims=True) * EXP2_SCALE

        def weights(j, norm):
            tile = jnp.exp2(s_ref[j] * EXP2_SCALE - peak)
            s_ref[j] = tile
            return norm + fold(tile, jnp.sum)

        norm = lax.fori_loop(begin, c + 1, weights, jnp.zeros((8, QROWS), jnp.float32))
        inverse = 1.0 / jnp.sum(norm, axis=0, keepdims=True)
        stat_ref[c, 0:1, :] = peak
        stat_ref[c, 1:2, :] = inverse
        ot_ref[...] = jnp.zeros_like(ot_ref)

        def attended(j, carry):
            ot_ref[...] += dot(vt_ref[j], low(s_ref[j] * inverse))
            return carry

        lax.fori_loop(begin, c + 1, attended, 0)
        out_low = low(ot_ref[...])
        for h in range(RATIO):
            part = dot_nt(eye_hd, out_low[:, h * 128 : (h + 1) * 128])
            wide_ref[:, unit_rows(c), h * HD : (h + 1) * HD] = part.reshape(SPAN, 8, HD)
        return carry

    lax.fori_loop(0, UNITS, one_unit, 0)
    o_ref[...] = low(wide_ref[...])


def forward(info, arrived, kv_oth):
    return pl.pallas_call(
        forward_kernel,
        in_specs=[SMEM, VMEM, VMEM],
        out_specs=[VMEM] * 5,
        out_shape=[
            shape((SPAN, 64, RATIO * HD)),
            shape((UNITS, QROWS, HD)),
            shape((UNITS, 256, HD)),
            shape((UNITS, 256, HD)),
            shape((UNITS, 8, QROWS), jnp.float32),
        ],
        scratch_shapes=[
            pltpu.VMEM((UNITS, HD, 256), jnp.bfloat16),
            pltpu.VMEM((UNITS, 256, QROWS), jnp.float32),
            pltpu.VMEM((256, QROWS), jnp.float32),
            pltpu.VMEM((HD, QROWS), jnp.float32),
            pltpu.VMEM((SPAN, 64, RATIO * HD), jnp.float32),
        ],
        compiler_params=pltpu.CompilerParams(vmem_limit_bytes=60 * MIB),
        cost_estimate=pl.CostEstimate(
            flops=5_000_000_000, bytes_accessed=8_000_000, transcendentals=5_000_000
        ),
        name="attend_forward",
    )(info, arrived, kv_oth)


def backward_kernel(
    info_ref, x_ref, q_ref, k_ref, v_ref, o_ref, stat_ref, dq_ref, own_ref, oth_ref, g_ref, kt_ref, bias_ref, dk_ref, dv_ref, dqt_ref, wide_ref, owide_ref
):
    core, first_len = place(info_ref)
    order = take_order()
    bias_ref[...] = causal_bias(core)
    owide_ref[...] = o_ref[...].astype(jnp.float32)
    for part in range(SPAN // 2):
        place_heads(sort_rows(order, x_ref, part), part, g_ref)
    eye_hd = eye(HD)
    for c in range(UNITS):
        kt_ref[c] = low(dot_nt(eye_hd, k_ref[c]))
    dk_ref[...] = jnp.zeros_like(dk_ref)
    dv_ref[...] = jnp.zeros_like(dv_ref)

    def one_unit(c, carry):
        begin = jnp.where(c < first_len, 0, first_len)
        q4, g4 = q_ref[c], g_ref[c]
        out = low(owide_ref[:, unit_rows(c), :].reshape(128, RATIO * HD))
        delta = jnp.concatenate(
            [
                jnp.sum(
                    dot_nt(eye_hd, out[:, h * HD : (h + 1) * HD])
                    * dot_nt(eye_hd, g4[h * 128 : (h + 1) * 128]),
                    axis=0,
                    keepdims=True,
                )
                for h in range(RATIO)
            ],
            axis=1,
        )
        peak, inverse = stat_ref[c, 0:1, :], stat_ref[c, 1:2, :]
        dqt_ref[...] = jnp.zeros_like(dqt_ref)

        def tile(j, tile_scores):
            probs = jnp.exp2(tile_scores * EXP2_SCALE - peak) * inverse
            dv_ref[j] += dot(low(probs), g4)
            dscores = low(probs * (dot_nt(v_ref[j], g4) - delta))
            dk_ref[j] += dot(dscores, q4)
            dqt_ref[...] += dot(kt_ref[j], dscores)

        def full(j, carry):
            tile(j, dot_nt(k_ref[j], q4))
            return carry

        lax.fori_loop(begin, c, full, 0)
        tile(c, dot_nt(k_ref[c], q4) + bias_ref[...])
        dq_low = low(dqt_ref[...] * SCALE)
        for h in range(RATIO):
            part = dot_nt(eye_hd, dq_low[:, h * 128 : (h + 1) * 128])
            wide_ref[:, unit_rows(c), h * HD : (h + 1) * HD] = part.reshape(SPAN, 8, HD)
        return carry

    lax.fori_loop(0, UNITS, one_unit, 0)
    dq_ref[...] = low(wide_ref[...])
    for c in range(UNITS):
        rows = slice(c * 8, (c + 1) * 8)
        own_ref[:, rows, 0:HD] = (dk_ref[c, 0:128] * SCALE).reshape(SPAN, 8, HD)
        own_ref[:, rows, HD:] = dv_ref[c, 0:128].reshape(SPAN, 8, HD)
        wide_ref[:, rows, 0:HD] = (dk_ref[c, 128:] * SCALE).reshape(SPAN, 8, HD)
        wide_ref[:, rows, HD : 2 * HD] = dv_ref[c, 128:].reshape(SPAN, 8, HD)
    oth_ref[...] = low(wide_ref[:, :, 0 : 2 * HD])


def backward(info, qg, q, k, v, out, stats):
    return pl.pallas_call(
        backward_kernel,
        in_specs=[SMEM] + [VMEM] * 6,
        out_specs=[VMEM] * 3,
        out_shape=[
            shape((SPAN, 64, RATIO * HD)),
            shape((SPAN, 64, 2 * HD), jnp.float32),
            shape((SPAN, 64, 2 * HD)),
        ],
        scratch_shapes=[
            pltpu.VMEM((UNITS, QROWS, HD), jnp.bfloat16),
            pltpu.VMEM((UNITS, HD, 256), jnp.bfloat16),
            pltpu.VMEM((256, QROWS), jnp.float32),
            pltpu.VMEM((UNITS, 256, HD), jnp.float32),
            pltpu.VMEM((UNITS, 256, HD), jnp.float32),
            pltpu.VMEM((HD, QROWS), jnp.float32),
            pltpu.VMEM((SPAN, 64, RATIO * HD), jnp.float32),
            pltpu.VMEM((SPAN, 64, RATIO * HD), jnp.float32),
        ],
        compiler_params=pltpu.CompilerParams(vmem_limit_bytes=60 * MIB),
        cost_estimate=pl.CostEstimate(
            flops=12_000_000_000, bytes_accessed=8_000_000, transcendentals=5_000_000
        ),
        name="attend_backward",
    )(info, qg, q, k, v, out, stats)


def join_kernel(dq_ref, own_ref, oth_ref, out_ref):
    out_ref[:, :, 0 : RATIO * HD] = dq_ref[...]
    out_ref[:, :, RATIO * HD :] = low(own_ref[...] + oth_ref[...].astype(jnp.float32))


def join(dq, own, oth):
    step = SPAN // 4

    def block(lanes):
        return pl.BlockSpec((step, 64, lanes), lambda i: (i, 0, 0))

    return pl.pallas_call(
        join_kernel,
        grid=(4,),
        in_specs=[block(RATIO * HD), block(2 * HD), block(2 * HD)],
        out_specs=block(6 * HD),
        out_shape=shape((SPAN, 64, 6 * HD)),
        compiler_params=pltpu.CompilerParams(vmem_limit_bytes=60 * MIB),
        name="join_gradients",
    )(dq, own, oth)


def row_order(core):
    row = lax.broadcasted_iota(jnp.int32, (128, 128), 0)
    col = lax.broadcasted_iota(jnp.int32, (128, 128), 1)
    other = jnp.where(row % 2 == core, 0, 64)
    return low(jnp.where(col == other + (row // 16) * 8 + (row % 16) // 2, 1.0, 0.0))


def unpack_kernel(widths, z_ref, oth_ref, *out_refs):
    core = lax.axis_index("core")
    order = row_order(core)
    for g in range(KVH):
        both = jnp.concatenate([z_ref[g, core], oth_ref[g]], axis=0)
        placed = low(dot(order, both))
        begin = 0
        for width, ref in zip(widths, out_refs):
            ref[:, g * width : (g + 1) * width] = placed[:, begin : begin + width]
            begin += width


def unpack(z, oth, widths):
    return pl.pallas_call(
        functools.partial(unpack_kernel, widths),
        in_specs=[VMEM, VMEM],
        out_specs=[VMEM] * len(widths),
        out_shape=[shape((128, KVH * width)) for width in widths],
        compiler_params=pltpu.CompilerParams(vmem_limit_bytes=24 * MIB),
        name="unpack_rows",
    )(z, oth)


def body(queries, keys, values, out_grad, doc_lengths, owner_docs):
    core = lax.axis_index("core")
    lengths = doc_lengths.T

    def swap(tensor):
        return lax.ppermute(tensor, "core", [(0, 1), (1, 0)])

    def spread(tensor):
        return lax.all_to_all(tensor, "sp", split_axis=0, concat_axis=0, tiled=True)

    def finish(tensor, widths):
        split = tensor.reshape((KVH, 2) + tensor.shape[1:])
        oth = swap(lax.dynamic_index_in_dim(split, 1 - core, 1, keepdims=False))
        return unpack(split, oth, widths)

    def gather(tensor):
        flat = tensor.reshape((BLOCKS * SPAN,) + tensor.shape[3:])
        moved = lax.all_to_all(flat, ("block", "sp"), split_axis=0, concat_axis=0, tiled=True)
        return moved.reshape((BLOCKS, SPAN) + tensor.shape[3:])

    qkv = gather(pack("pack_qkv", lengths, owner_docs, queries, keys, values))
    packed_grad = pack("pack_grad", lengths, owner_docs, out_grad)
    qkv, packed_grad = lax.optimization_barrier((qkv, packed_grad))
    grad = gather(packed_grad)
    kv_oth = swap(qkv[:, :, :, PAIR:])
    out, q, k, v, stats = forward(lengths, qkv, kv_oth)
    out, grad = lax.optimization_barrier((out, grad))
    out_back = spread(out)
    dq, own, oth = backward(lengths, grad, q, k, v, out, stats)
    dq, own, oth, out_back = lax.optimization_barrier((dq, own, oth, out_back))
    back = spread(join(dq, own, swap(oth)))
    (attn_out,) = finish(out_back, (RATIO * HD,))
    back, attn_out = lax.optimization_barrier((back, attn_out))
    return (attn_out, *finish(back, (RATIO * HD, HD, HD)))


def solution(mesh):
    cut = Mesh(mesh.devices.reshape(BLOCKS, 2, SPAN), ("block", "core", "sp"))
    rows = P(("block", "core", "sp"), None)
    return jax.shard_map(
        body,
        mesh=cut,
        in_specs=(rows, rows, rows, rows, P(), P()),
        out_specs=(rows, rows, rows, rows),
        check_vma=False,
    )
```

```python
import functools
import math

import jax
import jax.numpy as jnp
from jax import lax
from jax.experimental import pallas as pl
from jax.experimental.pallas import tpu as pltpu
from jax.sharding import Mesh
from jax.sharding import PartitionSpec as P

QH = 32
KVH = 8
HD = 128
GROUPS = 16
UNITS = 8
BLOCKS = 8
SPAN = 16
RATIO = QH // KVH
QROWS = RATIO * 128
PAIR = 2 * HD
LANES = PAIR + HD
PACK_STEP = 2
SCALE = 1.0 / math.sqrt(HD)
EXP2_SCALE = SCALE * math.log2(math.e)
NT = (((1,), (1,)), ((), ()))
MIB = 1024 * 1024
SMEM = pl.BlockSpec(memory_space=pltpu.SMEM)
VMEM = pl.BlockSpec(memory_space=pltpu.VMEM)


def shape(dims, kind=jnp.bfloat16):
    return jax.ShapeDtypeStruct(dims, kind)


def dot(left, right):
    return jnp.dot(left, right, preferred_element_type=jnp.float32)


def dot_nt(left, right):
    return lax.dot_general(left, right, NT, preferred_element_type=jnp.float32)


def low(value):
    return value.astype(jnp.bfloat16)


def eye(size):
    row = lax.broadcasted_iota(jnp.int32, (size, size), 0)
    col = lax.broadcasted_iota(jnp.int32, (size, size), 1)
    return low(jnp.where(row == col, 1.0, 0.0))


def take_order():
    row = lax.broadcasted_iota(jnp.int32, (256, 256), 0)
    col = lax.broadcasted_iota(jnp.int32, (256, 256), 1)
    wanted = (row % 2) * 128 + (row // 8 % 2) * 64 + (row // 2 % 4) * 16 + (row // 128) * 8
    wanted = wanted + (row // 16) % 8
    return low(jnp.where(col == wanted, 1.0, 0.0))


def select_rows(len_ref, own_ref, start_ref, sel_ref):
    def place(entry, total):
        doc = own_ref[entry]
        start_ref[doc] = total
        return total + len_ref[doc % 2, doc // 2]

    lax.fori_loop(0, 2 * GROUPS, place, jnp.int32(0))
    unit = lax.broadcasted_iota(jnp.int32, (UNITS, 128), 0)
    column = lax.broadcasted_iota(jnp.int32, (UNITS, 128), 1)
    for b in range(GROUPS):
        first = len_ref[0, b]
        source = jnp.where(
            unit < first, start_ref[2 * b] + unit, start_ref[2 * b + 1] + unit - first
        )
        sel_ref[b * UNITS : (b + 1) * UNITS, :] = jnp.where(column == source, 1.0, 0.0)


def pack_kernel(len_ref, own_ref, wide_ref, *refs):
    (*narrow_refs, out_ref, start_ref, sel_ref) = refs

    @pl.when(pl.program_id(0) == 0)
    def _():
        select_rows(len_ref, own_ref, start_ref, sel_ref)

    sel = low(sel_ref[...])

    def pick(ref):
        return dot(sel, ref[...]).reshape(GROUPS, UNITS, ref.shape[1])

    wide = pick(wide_ref)
    narrow = [pick(ref) for ref in narrow_refs]
    for i in range(PACK_STEP):
        begin = i * RATIO * HD
        first, second = wide[:, :, begin : begin + PAIR], wide[:, :, begin + PAIR : begin + 2 * PAIR]
        parts = [(0, low(jnp.concatenate([first, second], axis=1)))]
        if narrow:
            both = low(jnp.concatenate([n[:, :, i * HD : (i + 1) * HD] for n in narrow], axis=1))
            parts.append((PAIR, both))
        for lane, both in parts:
            lanes = slice(lane, lane + both.shape[2])
            both = both.reshape(4, 2, 2, 16, both.shape[2])
            for h in range(2):
                for y in range(2):
                    out_ref[0, h, 2 * i + y, :, :, lanes] = both[:, h, y]


def pack(name, lengths, owner_docs, wide, *narrow):
    lanes = PAIR + (HD if narrow else 0)
    return pl.pallas_call(
        pack_kernel,
        grid=(KVH // PACK_STEP,),
        in_specs=[SMEM, SMEM, pl.BlockSpec((128, PACK_STEP * RATIO * HD), lambda i: (0, i))]
        + [pl.BlockSpec((128, PACK_STEP * HD), lambda i: (0, i)) for _ in narrow],
        out_specs=pl.BlockSpec((1, 2, 4, 4, 16, lanes), lambda i: (i, 0, 0, 0, 0, 0)),
        out_shape=shape((4, 2, 4, 4, 16, lanes)),
        scratch_shapes=[pltpu.SMEM((2 * GROUPS,), jnp.int32), pltpu.VMEM((128, 128), jnp.float32)],
        compiler_params=pltpu.CompilerParams(vmem_limit_bytes=56 * MIB),
        name=name,
    )(lengths, owner_docs, wide, *narrow)


def fold(tile, how):
    return how(tile.reshape(tile.shape[0] // 8, 8, tile.shape[1]), axis=0)


def place(len_ref):
    group = lax.axis_index("x") * 4 + lax.axis_index("zh") * 2 + lax.axis_index("y") % 2
    return lax.axis_index("core"), len_ref[0, group]


def causal_bias(core):
    key = lax.broadcasted_iota(jnp.int32, (256, QROWS), 0)
    query = lax.broadcasted_iota(jnp.int32, (256, QROWS), 1)
    key_core = jnp.where(key < 128, core, 1 - core)
    key_pos = (key % 8) * 32 + key_core * 16 + (key // 8) % SPAN
    query_pos = (query % 8) * 32 + core * 16 + (query // 8) % SPAN
    return jnp.where(key_pos <= query_pos, 0.0, -1e30)


def sort_rows(order, ref, part):
    y = 2 * (part % 2)
    rows = ref[part // 2, :, y : y + 2]
    return low(dot(order, rows.reshape(256, rows.shape[4])))


def place_heads(placed, part, ref):
    for h in range(RATIO):
        here = slice(h * 128 + part * 16, h * 128 + (part + 1) * 16)
        row, lane = (h // 2) * 128, (h % 2) * HD
        ref[:, here, :] = placed[row : row + 128, lane : lane + HD].reshape(UNITS, 16, HD)


def unit_rows(c):
    return pl.ds(pl.multiple_of(c * 8, 8), 8)


def forward_kernel(
    info_ref, x_ref, oth_ref, o_ref, q_ref, k_ref, v_ref, stat_ref, vt_ref, s_ref, bias_ref, ot_ref, wide_ref
):
    core, first_len = place(info_ref)
    order = take_order()
    bias_ref[...] = causal_bias(core)
    for part in range(SPAN // 2):
        own = sort_rows(order, x_ref, part)
        place_heads(own, part, q_ref)
        for base, placed in ((0, own[:, PAIR:]), (128, sort_rows(order, oth_ref, part))):
            here = slice(base + part * 16, base + (part + 1) * 16)
            k_ref[:, here, :] = placed[:128].reshape(UNITS, 16, HD)
            v_ref[:, here, :] = placed[128:].reshape(UNITS, 16, HD)
    eye_hd = eye(HD)
    for c in range(UNITS):
        vt_ref[c] = low(dot_nt(eye_hd, v_ref[c]))

    def one_unit(base, r):
        c = base + r
        q4 = q_ref[c]

        def attend_units(units):
            peak = None
            for i, j in enumerate(units):
                tile = dot_nt(k_ref[j], q4)
                if i == len(units) - 1:
                    tile = tile + bias_ref[...]
                s_ref[i] = tile
                top = fold(tile, jnp.max)
                peak = top if peak is None else jnp.maximum(peak, top)
            peak = jnp.max(peak, axis=0, keepdims=True) * EXP2_SCALE
            norm = jnp.zeros((8, QROWS), jnp.float32)
            for i in range(len(units)):
                tile = jnp.exp2(s_ref[i] * EXP2_SCALE - peak)
                s_ref[i] = tile
                norm = norm + fold(tile, jnp.sum)
            norm = jnp.sum(norm, axis=0, keepdims=True)
            inverse = 1.0 / norm
            stat_ref[c, 0:1, :] = peak + jnp.log2(norm)
            ot_ref[...] = sum(dot(vt_ref[j], low(s_ref[i] * inverse)) for i, j in enumerate(units))

        own = [base + j for j in range(r + 1)]
        whole = jnp.logical_and(base > 0, first_len > UNITS // 2)
        pl.when(whole)(lambda: attend_units(list(range(UNITS // 2)) + own))
        pl.when(jnp.logical_not(whole))(lambda: attend_units(own))
        out_low = low(ot_ref[...])
        for h in range(RATIO):
            part = dot_nt(eye_hd, out_low[:, h * 128 : (h + 1) * 128])
            wide_ref[:, unit_rows(c), h * HD : (h + 1) * HD] = part.reshape(SPAN, 8, HD)

    def one_half(half, carry):
        for r in range(UNITS // 2):
            one_unit(half * (UNITS // 2), r)
        return carry

    lax.fori_loop(0, 2, one_half, 0)
    o_ref[...] = low(wide_ref[...])


def forward(info, arrived, kv_oth):
    return pl.pallas_call(
        forward_kernel,
        in_specs=[SMEM, VMEM, VMEM],
        out_specs=[VMEM] * 5,
        out_shape=[
            shape((SPAN, 64, RATIO * HD)),
            shape((UNITS, QROWS, HD)),
            shape((UNITS, 256, HD)),
            shape((UNITS, 256, HD)),
            shape((UNITS, 8, QROWS), jnp.float32),
        ],
        scratch_shapes=[
            pltpu.VMEM((UNITS, HD, 256), jnp.bfloat16),
            pltpu.VMEM((UNITS, 256, QROWS), jnp.float32),
            pltpu.VMEM((256, QROWS), jnp.float32),
            pltpu.VMEM((HD, QROWS), jnp.float32),
            pltpu.VMEM((SPAN, 64, RATIO * HD), jnp.float32),
        ],
        compiler_params=pltpu.CompilerParams(vmem_limit_bytes=60 * MIB),
        cost_estimate=pl.CostEstimate(
            flops=5_000_000_000, bytes_accessed=8_000_000, transcendentals=5_000_000
        ),
        name="attend_forward",
    )(info, arrived, kv_oth)


def backward_kernel(
    info_ref, x_ref, q_ref, k_ref, v_ref, o_ref, stat_ref, grad_ref, oth_ref, g_ref, kt_ref, bias_ref, dk_ref, dv_ref, dqt_ref, wide_ref, owide_ref
):
    core, first_len = place(info_ref)
    order = take_order()
    bias_ref[...] = causal_bias(core)
    owide_ref[...] = o_ref[...].astype(jnp.float32)
    for part in range(SPAN // 2):
        place_heads(sort_rows(order, x_ref, part), part, g_ref)
    eye_hd = eye(HD)
    for c in range(UNITS):
        kt_ref[c] = low(dot_nt(eye_hd, k_ref[c]))
    dk_ref[...] = jnp.zeros_like(dk_ref)
    dv_ref[...] = jnp.zeros_like(dv_ref)

    def one_unit(base, r):
        c = base + r
        q4, g4 = q_ref[c], g_ref[c]
        out = low(owide_ref[:, unit_rows(c), :].reshape(128, RATIO * HD))
        delta = jnp.concatenate(
            [
                jnp.sum(
                    dot_nt(eye_hd, out[:, h * HD : (h + 1) * HD])
                    * dot_nt(eye_hd, g4[h * 128 : (h + 1) * 128]),
                    axis=0,
                    keepdims=True,
                )
                for h in range(RATIO)
            ],
            axis=1,
        )
        level = stat_ref[c, 0:1, :]

        def tiles(units, diagonal):
            scores = [dot_nt(k_ref[j], q4) for j in units]
            if diagonal:
                scores[-1] = scores[-1] + bias_ref[...]
            probs = [jnp.exp2(tile * EXP2_SCALE - level) for tile in scores]
            dprobs = [dot_nt(v_ref[j], g4) for j in units]
            dscores = [low(p * (d - delta)) for p, d in zip(probs, dprobs)]
            for j, p, d in zip(units, probs, dscores):
                dv_ref[j] += dot(low(p), g4)
                dk_ref[j] += dot(d, q4)
            return sum(dot(kt_ref[j], d) for j, d in zip(units, dscores))

        own = [base + j for j in range(r + 1)]
        if r >= 2:
            dqt_ref[...] = tiles(own[:-2], False) + tiles(own[-2:], True)
        else:
            dqt_ref[...] = tiles(own, True)

        @pl.when(jnp.logical_and(base > 0, first_len > UNITS // 2))
        def _():
            dqt_ref[...] += tiles([0, 1], False) + tiles([2, 3], False)

        dq_low = low(dqt_ref[...] * SCALE)
        for h in range(RATIO):
            part = dot_nt(eye_hd, dq_low[:, h * 128 : (h + 1) * 128])
            wide_ref[:, unit_rows(c), h * HD : (h + 1) * HD] = part.reshape(SPAN, 8, HD)

    def one_half(half, carry):
        for r in range(UNITS // 2):
            one_unit(half * (UNITS // 2), r)
        return carry

    lax.fori_loop(0, 2, one_half, 0)
    grad_ref[:, :, 0 : RATIO * HD] = low(wide_ref[...])
    for c in range(UNITS):
        rows = slice(c * 8, (c + 1) * 8)
        for i in range(2):
            keys = slice(i * 128, (i + 1) * 128)
            lane = i * 2 * HD
            wide_ref[:, rows, lane : lane + HD] = (dk_ref[c, keys] * SCALE).reshape(SPAN, 8, HD)
            wide_ref[:, rows, lane + HD : lane + 2 * HD] = dv_ref[c, keys].reshape(SPAN, 8, HD)
    grad_ref[:, :, RATIO * HD :] = low(wide_ref[:, :, 0 : 2 * HD])
    oth_ref[...] = low(wide_ref[:, :, 2 * HD :])


def backward(info, qg, q, k, v, out, stats):
    return pl.pallas_call(
        backward_kernel,
        in_specs=[SMEM] + [VMEM] * 6,
        out_specs=[VMEM] * 2,
        out_shape=[
            shape((SPAN, 64, 6 * HD)),
            shape((SPAN, 64, 2 * HD)),
        ],
        scratch_shapes=[
            pltpu.VMEM((UNITS, QROWS, HD), jnp.bfloat16),
            pltpu.VMEM((UNITS, HD, 256), jnp.bfloat16),
            pltpu.VMEM((256, QROWS), jnp.float32),
            pltpu.VMEM((UNITS, 256, HD), jnp.float32),
            pltpu.VMEM((UNITS, 256, HD), jnp.float32),
            pltpu.VMEM((HD, QROWS), jnp.float32),
            pltpu.VMEM((SPAN, 64, RATIO * HD), jnp.float32),
            pltpu.VMEM((SPAN, 64, RATIO * HD), jnp.float32),
        ],
        compiler_params=pltpu.CompilerParams(vmem_limit_bytes=60 * MIB),
        cost_estimate=pl.CostEstimate(
            flops=12_000_000_000, bytes_accessed=8_000_000, transcendentals=5_000_000
        ),
        name="attend_backward",
    )(info, qg, q, k, v, out, stats)


def join_kernel(own_ref, oth_ref, out_ref):
    out_ref[...] = low(own_ref[...].astype(jnp.float32) + oth_ref[...].astype(jnp.float32))


def join(gradients, oth):
    step = SPAN // 4
    block = (step, 64, 2 * HD)
    return pl.pallas_call(
        join_kernel,
        grid=(4,),
        in_specs=[
            pl.BlockSpec(block, lambda i: (i, 0, 2)),
            pl.BlockSpec(block, lambda i: (i, 0, 0)),
        ],
        out_specs=pl.BlockSpec(block, lambda i: (i, 0, 2)),
        out_shape=shape((SPAN, 64, 6 * HD)),
        input_output_aliases={0: 0},
        compiler_params=pltpu.CompilerParams(vmem_limit_bytes=60 * MIB),
        name="join_gradients",
    )(gradients, oth)


def row_order(core):
    row = lax.broadcasted_iota(jnp.int32, (128, 128), 0)
    col = lax.broadcasted_iota(jnp.int32, (128, 128), 1)
    other = jnp.where(row % 2 == core, 0, 64)
    return low(jnp.where(col == other + (row // 16) * 8 + (row % 16) // 2, 1.0, 0.0))


def unpack_kernel(widths, z_ref, oth_ref, *out_refs):
    core = lax.axis_index("core")
    order = row_order(core)
    for g in range(KVH):
        both = jnp.concatenate([z_ref[g, core], oth_ref[g]], axis=0)
        placed = low(dot(order, both))
        begin = 0
        for width, ref in zip(widths, out_refs):
            ref[:, g * width : (g + 1) * width] = placed[:, begin : begin + width]
            begin += width


def unpack(z, oth, widths):
    return pl.pallas_call(
        functools.partial(unpack_kernel, widths),
        in_specs=[VMEM, VMEM],
        out_specs=[VMEM] * len(widths),
        out_shape=[shape((128, KVH * width)) for width in widths],
        compiler_params=pltpu.CompilerParams(vmem_limit_bytes=24 * MIB),
        name="unpack_rows",
    )(z, oth)


def body(queries, keys, values, out_grad, doc_lengths, owner_docs):
    core = lax.axis_index("core")
    lengths = doc_lengths.T

    def swap(tensor):
        return lax.ppermute(tensor, "core", [(0, 1), (1, 0)])

    def spread(tensor):
        return lax.all_to_all(tensor, ("zl", "y"), split_axis=0, concat_axis=0, tiled=True)

    def finish(tensor, widths):
        split = tensor.reshape((KVH, 2) + tensor.shape[1:])
        oth = swap(lax.dynamic_index_in_dim(split, 1 - core, 1, keepdims=False))
        return unpack(split, oth, widths)

    def gather(tensor):
        flat = tensor.reshape((BLOCKS * SPAN,) + tensor.shape[4:])
        moved = lax.all_to_all(flat, ("zl", "zh", "y", "x"), split_axis=0, concat_axis=0, tiled=True)
        return moved.reshape(tensor.shape)

    qkv = gather(pack("pack_qkv", lengths, owner_docs, queries, keys, values))
    packed_grad = pack("pack_grad", lengths, owner_docs, out_grad)
    qkv, packed_grad = lax.optimization_barrier((qkv, packed_grad))
    grad = gather(packed_grad)
    kv_oth = swap(qkv[..., PAIR:])
    out, q, k, v, stats = forward(lengths, qkv, kv_oth)
    out, grad = lax.optimization_barrier((out, grad))
    out_back = spread(out)
    gradients, oth = backward(lengths, grad, q, k, v, out, stats)
    gradients = join(gradients, swap(oth))
    gradients, out_back = lax.optimization_barrier((gradients, out_back))
    back = spread(gradients)
    (attn_out,) = finish(out_back, (RATIO * HD,))
    back, attn_out = lax.optimization_barrier((back, attn_out))
    return (attn_out, *finish(back, (RATIO * HD, HD, HD)))


def solution(mesh):
    cut = Mesh(mesh.devices.reshape(4, 2, 2, 4, 4), ("x", "zh", "core", "zl", "y"))
    rows = P(("x", "zh", "core", "zl", "y"), None)
    return jax.shard_map(
        body,
        mesh=cut,
        in_specs=(rows, rows, rows, rows, P(), P()),
        out_specs=(rows, rows, rows, rows),
        check_vma=False,
    )
```

```python
import functools
import math

import jax
import jax.numpy as jnp
from jax import lax
from jax.experimental import pallas as pl
from jax.experimental.pallas import tpu as pltpu
from jax.sharding import Mesh
from jax.sharding import PartitionSpec as P

QH = 32
KVH = 8
HD = 128
GROUPS = 16
UNITS = 8
BLOCKS = 8
SPAN = 16
RATIO = QH // KVH
QROWS = RATIO * 128
PAIR = 2 * HD
LANES = PAIR + HD
PACK_STEP = 4
SCALE = 1.0 / math.sqrt(HD)
EXP2_SCALE = SCALE * math.log2(math.e)
NT = (((1,), (1,)), ((), ()))
MIB = 1024 * 1024
SMEM = pl.BlockSpec(memory_space=pltpu.SMEM)
VMEM = pl.BlockSpec(memory_space=pltpu.VMEM)


def shape(dims, kind=jnp.bfloat16):
    return jax.ShapeDtypeStruct(dims, kind)


def dot(left, right):
    return jnp.dot(left, right, preferred_element_type=jnp.float32)


def dot_nt(left, right):
    return lax.dot_general(left, right, NT, preferred_element_type=jnp.float32)


def low(value):
    return value.astype(jnp.bfloat16)


def eye(size):
    row = lax.broadcasted_iota(jnp.int32, (size, size), 0)
    col = lax.broadcasted_iota(jnp.int32, (size, size), 1)
    return low(jnp.where(row == col, 1.0, 0.0))


def take_order():
    row = lax.broadcasted_iota(jnp.int32, (256, 256), 0)
    col = lax.broadcasted_iota(jnp.int32, (256, 256), 1)
    wanted = (row % 2) * 128 + (row // 8 % 2) * 64 + (row // 2 % 4) * 16 + (row // 128) * 8
    wanted = wanted + (row // 16) % 8
    return low(jnp.where(col == wanted, 1.0, 0.0))


def select_rows(len_ref, own_ref, start_ref, sel_ref):
    def place(entry, total):
        doc = own_ref[entry]
        start_ref[doc] = total
        return total + len_ref[doc % 2, doc // 2]

    lax.fori_loop(0, 2 * GROUPS, place, jnp.int32(0))
    unit = lax.broadcasted_iota(jnp.int32, (UNITS, 128), 0)
    column = lax.broadcasted_iota(jnp.int32, (UNITS, 128), 1)
    for b in range(GROUPS):
        first = len_ref[0, b]
        source = jnp.where(
            unit < first, start_ref[2 * b] + unit, start_ref[2 * b + 1] + unit - first
        )
        sel_ref[b * UNITS : (b + 1) * UNITS, :] = jnp.where(column == source, 1.0, 0.0)


def pack_kernel(len_ref, own_ref, wide_ref, *refs):
    (*narrow_refs, out_ref, start_ref, sel_ref) = refs

    @pl.when(pl.program_id(0) == 0)
    def _():
        select_rows(len_ref, own_ref, start_ref, sel_ref)

    sel = low(sel_ref[...])

    def pick(ref):
        return dot(sel, ref[...]).reshape(GROUPS, UNITS, ref.shape[1])

    wide = pick(wide_ref)
    narrow = [pick(ref) for ref in narrow_refs]
    for i in range(PACK_STEP):
        begin = i * RATIO * HD
        first, second = wide[:, :, begin : begin + PAIR], wide[:, :, begin + PAIR : begin + 2 * PAIR]
        parts = [(0, low(jnp.concatenate([first, second], axis=1)))]
        if narrow:
            both = low(jnp.concatenate([n[:, :, i * HD : (i + 1) * HD] for n in narrow], axis=1))
            parts.append((PAIR, both))
        for lane, both in parts:
            lanes = slice(lane, lane + both.shape[2])
            both = both.reshape(4, 2, 2, 16, both.shape[2])
            for h in range(2):
                for y in range(2):
                    out_ref[i // 2, h, 2 * (i % 2) + y, :, :, lanes] = both[:, h, y]


def pack(name, lengths, owner_docs, wide, *narrow):
    lanes = PAIR + (HD if narrow else 0)
    return pl.pallas_call(
        pack_kernel,
        grid=(KVH // PACK_STEP,),
        in_specs=[SMEM, SMEM, pl.BlockSpec((128, PACK_STEP * RATIO * HD), lambda i: (0, i))]
        + [pl.BlockSpec((128, PACK_STEP * HD), lambda i: (0, i)) for _ in narrow],
        out_specs=pl.BlockSpec((PACK_STEP // 2, 2, 4, 4, 16, lanes), lambda i: (i, 0, 0, 0, 0, 0)),
        out_shape=shape((4, 2, 4, 4, 16, lanes)),
        scratch_shapes=[pltpu.SMEM((2 * GROUPS,), jnp.int32), pltpu.VMEM((128, 128), jnp.float32)],
        compiler_params=pltpu.CompilerParams(vmem_limit_bytes=56 * MIB),
        name=name,
    )(lengths, owner_docs, wide, *narrow)


def fold(tile, how):
    return how(tile.reshape(tile.shape[0] // 8, 8, tile.shape[1]), axis=0)


def place(len_ref):
    group = lax.axis_index("x") * 4 + lax.axis_index("zh") * 2 + lax.axis_index("y") % 2
    return lax.axis_index("core"), len_ref[0, group]


def causal_bias(core):
    key = lax.broadcasted_iota(jnp.int32, (256, QROWS), 0)
    query = lax.broadcasted_iota(jnp.int32, (256, QROWS), 1)
    key_core = jnp.where(key < 128, core, 1 - core)
    key_pos = (key % 8) * 32 + key_core * 16 + (key // 8) % SPAN
    query_pos = (query % 8) * 32 + core * 16 + (query // 8) % SPAN
    return jnp.where(key_pos <= query_pos, 0.0, -1e30)


def sort_rows(order, ref, part):
    y = 2 * (part % 2)
    rows = ref[part // 2, :, y : y + 2]
    return low(dot(order, rows.reshape(256, rows.shape[4])))


def place_heads(placed, part, ref):
    for h in range(RATIO):
        here = slice(h * 128 + part * 16, h * 128 + (part + 1) * 16)
        row, lane = (h // 2) * 128, (h % 2) * HD
        ref[:, here, :] = placed[row : row + 128, lane : lane + HD].reshape(UNITS, 16, HD)


def unit_rows(c):
    return pl.ds(pl.multiple_of(c * 8, 8), 8)


def forward_kernel(
    info_ref, x_ref, oth_ref, o_ref, q_ref, k_ref, v_ref, stat_ref, turned_ref, kt_ref, vt_ref, s_ref, bias_ref, ot_ref, wide_ref
):
    core, first_len = place(info_ref)
    order = take_order()
    bias_ref[...] = causal_bias(core)
    for part in range(SPAN // 2):
        own = sort_rows(order, x_ref, part)
        place_heads(own, part, q_ref)
        for base, placed in ((0, own[:, PAIR:]), (128, sort_rows(order, oth_ref, part))):
            here = slice(base + part * 16, base + (part + 1) * 16)
            k_ref[:, here, :] = placed[:128].reshape(UNITS, 16, HD)
            v_ref[:, here, :] = placed[128:].reshape(UNITS, 16, HD)
    eye_hd = eye(HD)
    for c in range(UNITS):
        vt_ref[c] = low(dot_nt(eye_hd, v_ref[c]))
        kt_ref[c] = low(dot_nt(eye_hd, k_ref[c]))

    def one_unit(base, r):
        c = base + r
        q4 = q_ref[c]

        def attend_units(units):
            peak = None
            for i, j in enumerate(units):
                tile = dot_nt(k_ref[j], q4)
                if i == len(units) - 1:
                    tile = tile + bias_ref[...]
                s_ref[i] = tile
                top = fold(tile, jnp.max)
                peak = top if peak is None else jnp.maximum(peak, top)
            peak = jnp.max(peak, axis=0, keepdims=True) * EXP2_SCALE
            norm = jnp.zeros((8, QROWS), jnp.float32)
            for i in range(len(units)):
                tile = jnp.exp2(s_ref[i] * EXP2_SCALE - peak)
                s_ref[i] = tile
                norm = norm + fold(tile, jnp.sum)
            norm = jnp.sum(norm, axis=0, keepdims=True)
            inverse = 1.0 / norm
            stat_ref[c, 0:1, :] = peak + jnp.log2(norm)
            ot_ref[...] = sum(dot(vt_ref[j], low(s_ref[i] * inverse)) for i, j in enumerate(units))

        own = [base + j for j in range(r + 1)]
        whole = jnp.logical_and(base > 0, first_len > UNITS // 2)
        pl.when(whole)(lambda: attend_units(list(range(UNITS // 2)) + own))
        pl.when(jnp.logical_not(whole))(lambda: attend_units(own))
        out_low = low(ot_ref[...])
        turned_ref[c] = out_low
        for h in range(RATIO):
            part = dot_nt(eye_hd, out_low[:, h * 128 : (h + 1) * 128])
            wide_ref[:, unit_rows(c), h * HD : (h + 1) * HD] = part.reshape(SPAN, 8, HD)

    def one_half(half, carry):
        for r in range(UNITS // 2):
            one_unit(half * (UNITS // 2), r)
        return carry

    lax.fori_loop(0, 2, one_half, 0)
    o_ref[...] = low(wide_ref[...])


def forward(info, arrived, kv_oth):
    return pl.pallas_call(
        forward_kernel,
        in_specs=[SMEM, VMEM, VMEM],
        out_specs=[VMEM] * 7,
        out_shape=[
            shape((SPAN, 64, RATIO * HD)),
            shape((UNITS, QROWS, HD)),
            shape((UNITS, 256, HD)),
            shape((UNITS, 256, HD)),
            shape((UNITS, 8, QROWS), jnp.float32),
            shape((UNITS, HD, QROWS)),
            shape((UNITS, HD, 256)),
        ],
        scratch_shapes=[
            pltpu.VMEM((UNITS, HD, 256), jnp.bfloat16),
            pltpu.VMEM((UNITS, 256, QROWS), jnp.float32),
            pltpu.VMEM((256, QROWS), jnp.float32),
            pltpu.VMEM((HD, QROWS), jnp.float32),
            pltpu.VMEM((SPAN, 64, RATIO * HD), jnp.float32),
        ],
        compiler_params=pltpu.CompilerParams(vmem_limit_bytes=60 * MIB),
        cost_estimate=pl.CostEstimate(
            flops=5_000_000_000, bytes_accessed=8_000_000, transcendentals=5_000_000
        ),
        name="attend_forward",
    )(info, arrived, kv_oth)


def backward_kernel(
    info_ref, x_ref, q_ref, k_ref, v_ref, stat_ref, turned_ref, kt_ref, grad_ref, oth_ref, g_ref, bias_ref, dk_ref, dv_ref, dqt_ref, wide_ref
):
    core, first_len = place(info_ref)
    order = take_order()
    bias_ref[...] = causal_bias(core)
    for part in range(SPAN // 2):
        place_heads(sort_rows(order, x_ref, part), part, g_ref)
    eye_hd = eye(HD)
    dk_ref[...] = jnp.zeros_like(dk_ref)
    dv_ref[...] = jnp.zeros_like(dv_ref)

    def one_unit(base, r):
        c = base + r
        q4, g4 = q_ref[c], g_ref[c]
        delta = jnp.sum(
            turned_ref[c].astype(jnp.float32) * dot_nt(eye_hd, g4), axis=0, keepdims=True
        )
        level = stat_ref[c, 0:1, :]

        def tiles(units, diagonal):
            scores = [dot_nt(k_ref[j], q4) for j in units]
            if diagonal:
                scores[-1] = scores[-1] + bias_ref[...]
            probs = [jnp.exp2(tile * EXP2_SCALE - level) for tile in scores]
            dprobs = [dot_nt(v_ref[j], g4) for j in units]
            dscores = [low(p * (d - delta)) for p, d in zip(probs, dprobs)]
            for j, p, d in zip(units, probs, dscores):
                dv_ref[j] += dot(low(p), g4)
                dk_ref[j] += dot(d, q4)
            return sum(dot(kt_ref[j], d) for j, d in zip(units, dscores))

        own = [base + j for j in range(r + 1)]
        if r >= 2:
            dqt_ref[...] = tiles(own[:-2], False) + tiles(own[-2:], True)
        else:
            dqt_ref[...] = tiles(own, True)

        @pl.when(jnp.logical_and(base > 0, first_len > UNITS // 2))
        def _():
            dqt_ref[...] += tiles([0, 1], False) + tiles([2, 3], False)

        dq_low = low(dqt_ref[...] * SCALE)
        for h in range(RATIO):
            part = dot_nt(eye_hd, dq_low[:, h * 128 : (h + 1) * 128])
            wide_ref[:, unit_rows(c), h * HD : (h + 1) * HD] = part.reshape(SPAN, 8, HD)

    def one_half(half, carry):
        for r in range(UNITS // 2):
            one_unit(half * (UNITS // 2), r)
        return carry

    lax.fori_loop(0, 2, one_half, 0)
    grad_ref[:, :, 0 : RATIO * HD] = low(wide_ref[...])
    for c in range(UNITS):
        rows = slice(c * 8, (c + 1) * 8)
        for i in range(2):
            keys = slice(i * 128, (i + 1) * 128)
            lane = i * 2 * HD
            wide_ref[:, rows, lane : lane + HD] = (dk_ref[c, keys] * SCALE).reshape(SPAN, 8, HD)
            wide_ref[:, rows, lane + HD : lane + 2 * HD] = dv_ref[c, keys].reshape(SPAN, 8, HD)
    grad_ref[:, :, RATIO * HD :] = low(wide_ref[:, :, 0 : 2 * HD])
    oth_ref[...] = low(wide_ref[:, :, 2 * HD :])


def backward(info, grad, *saved):
    return pl.pallas_call(
        backward_kernel,
        in_specs=[SMEM] + [VMEM] * 7,
        out_specs=[VMEM] * 2,
        out_shape=[
            shape((SPAN, 64, 6 * HD)),
            shape((SPAN, 64, 2 * HD)),
        ],
        scratch_shapes=[
            pltpu.VMEM((UNITS, QROWS, HD), jnp.bfloat16),
            pltpu.VMEM((256, QROWS), jnp.float32),
            pltpu.VMEM((UNITS, 256, HD), jnp.float32),
            pltpu.VMEM((UNITS, 256, HD), jnp.float32),
            pltpu.VMEM((HD, QROWS), jnp.float32),
            pltpu.VMEM((SPAN, 64, RATIO * HD), jnp.float32),
        ],
        compiler_params=pltpu.CompilerParams(vmem_limit_bytes=60 * MIB),
        cost_estimate=pl.CostEstimate(
            flops=12_000_000_000, bytes_accessed=8_000_000, transcendentals=5_000_000
        ),
        name="attend_backward",
    )(info, grad, *saved)


def join_kernel(own_ref, oth_ref, out_ref):
    out_ref[...] = low(own_ref[...].astype(jnp.float32) + oth_ref[...].astype(jnp.float32))


def join(gradients, oth):
    step = SPAN // 2
    block = (step, 64, 2 * HD)
    return pl.pallas_call(
        join_kernel,
        grid=(2,),
        in_specs=[
            pl.BlockSpec(block, lambda i: (i, 0, 2)),
            pl.BlockSpec(block, lambda i: (i, 0, 0)),
        ],
        out_specs=pl.BlockSpec(block, lambda i: (i, 0, 2)),
        out_shape=shape((SPAN, 64, 6 * HD)),
        input_output_aliases={0: 0},
        compiler_params=pltpu.CompilerParams(vmem_limit_bytes=60 * MIB),
        name="join_gradients",
    )(gradients, oth)


def row_order(core):
    row = lax.broadcasted_iota(jnp.int32, (128, 128), 0)
    col = lax.broadcasted_iota(jnp.int32, (128, 128), 1)
    other = jnp.where(row % 2 == core, 0, 64)
    return low(jnp.where(col == other + (row // 16) * 8 + (row % 16) // 2, 1.0, 0.0))


def unpack_kernel(widths, z_ref, oth_ref, *out_refs):
    core = lax.axis_index("core")
    order = row_order(core)
    for g in range(KVH):
        both = jnp.concatenate([z_ref[g, core], oth_ref[g]], axis=0)
        placed = low(dot(order, both))
        begin = 0
        for width, ref in zip(widths, out_refs):
            ref[:, g * width : (g + 1) * width] = placed[:, begin : begin + width]
            begin += width


def unpack(z, oth, widths):
    return pl.pallas_call(
        functools.partial(unpack_kernel, widths),
        in_specs=[VMEM, VMEM],
        out_specs=[VMEM] * len(widths),
        out_shape=[shape((128, KVH * width)) for width in widths],
        compiler_params=pltpu.CompilerParams(vmem_limit_bytes=24 * MIB),
        name="unpack_rows",
    )(z, oth)


def body(queries, keys, values, out_grad, doc_lengths, owner_docs):
    core = lax.axis_index("core")
    lengths = doc_lengths.T

    def swap(tensor):
        return lax.ppermute(tensor, "core", [(0, 1), (1, 0)])

    def spread(tensor):
        return lax.all_to_all(tensor, ("zl", "y"), split_axis=0, concat_axis=0, tiled=True)

    def finish(tensor, widths):
        split = tensor.reshape((KVH, 2) + tensor.shape[1:])
        oth = swap(lax.dynamic_index_in_dim(split, 1 - core, 1, keepdims=False))
        return unpack(split, oth, widths)

    def gather(tensor):
        flat = tensor.reshape((BLOCKS * SPAN,) + tensor.shape[4:])
        moved = lax.all_to_all(flat, ("zl", "zh", "y", "x"), split_axis=0, concat_axis=0, tiled=True)
        return moved.reshape(tensor.shape)

    qkv = gather(pack("pack_qkv", lengths, owner_docs, queries, keys, values))
    packed_grad = pack("pack_grad", lengths, owner_docs, out_grad)
    qkv, packed_grad = lax.optimization_barrier((qkv, packed_grad))
    grad = gather(packed_grad)
    kv_oth = swap(qkv[..., PAIR:])
    out, *saved = forward(lengths, qkv, kv_oth)
    out, grad = lax.optimization_barrier((out, grad))
    out_back = spread(out)
    gradients, oth = backward(lengths, grad, *saved)
    gradients = join(gradients, swap(oth))
    gradients, out_back = lax.optimization_barrier((gradients, out_back))
    back = spread(gradients)
    (attn_out,) = finish(out_back, (RATIO * HD,))
    back, attn_out = lax.optimization_barrier((back, attn_out))
    return (attn_out, *finish(back, (RATIO * HD, HD, HD)))


def solution(mesh):
    cut = Mesh(mesh.devices.reshape(4, 2, 2, 4, 4), ("x", "zh", "core", "zl", "y"))
    rows = P(("x", "zh", "core", "zl", "y"), None)
    return jax.shard_map(
        body,
        mesh=cut,
        in_specs=(rows, rows, rows, rows, P(), P()),
        out_specs=(rows, rows, rows, rows),
        check_vma=False,
    )
```

```python
import functools
import math

import jax
import jax.numpy as jnp
from jax import lax
from jax.experimental import pallas as pl
from jax.experimental.pallas import tpu as pltpu
from jax.sharding import Mesh
from jax.sharding import PartitionSpec as P

QH = 32
KVH = 8
HD = 128
GROUPS = 16
UNITS = 8
BLOCKS = 8
SPAN = 16
RATIO = QH // KVH
QROWS = RATIO * 128
PAIR = 2 * HD
LANES = PAIR + HD
PACK_STEP = 4
SCALE = 1.0 / math.sqrt(HD)
EXP2_SCALE = SCALE * math.log2(math.e)
NT = (((1,), (1,)), ((), ()))
MIB = 1024 * 1024
SMEM = pl.BlockSpec(memory_space=pltpu.SMEM)
VMEM = pl.BlockSpec(memory_space=pltpu.VMEM)


def shape(dims, kind=jnp.bfloat16):
    return jax.ShapeDtypeStruct(dims, kind)


def dot(left, right):
    return jnp.dot(left, right, preferred_element_type=jnp.float32)


def dot_nt(left, right):
    return lax.dot_general(left, right, NT, preferred_element_type=jnp.float32)


def low(value):
    return value.astype(jnp.bfloat16)


def eye(size):
    row = lax.broadcasted_iota(jnp.int32, (size, size), 0)
    col = lax.broadcasted_iota(jnp.int32, (size, size), 1)
    return low(jnp.where(row == col, 1.0, 0.0))


def take_order():
    row = lax.broadcasted_iota(jnp.int32, (256, 256), 0)
    col = lax.broadcasted_iota(jnp.int32, (256, 256), 1)
    wanted = (row % 2) * 128 + (row // 8 % 2) * 64 + (row // 2 % 4) * 16 + (row // 128) * 8
    wanted = wanted + (row // 16) % 8
    return low(jnp.where(col == wanted, 1.0, 0.0))


def select_rows(len_ref, own_ref, start_ref, sel_ref):
    docs = [own_ref[entry] for entry in range(2 * GROUPS)]
    sizes = [len_ref[doc & 1, doc >> 1] for doc in docs]
    total = jnp.int32(0)
    for doc, size in zip(docs, sizes):
        start_ref[doc] = total
        total = total + size
    unit = lax.broadcasted_iota(jnp.int32, (UNITS, 128), 0)
    column = lax.broadcasted_iota(jnp.int32, (UNITS, 128), 1)
    for b in range(GROUPS):
        first = len_ref[0, b]
        source = jnp.where(
            unit < first, start_ref[2 * b] + unit, start_ref[2 * b + 1] + unit - first
        )
        sel_ref[b * UNITS : (b + 1) * UNITS, :] = jnp.where(column == source, 1.0, 0.0)


def pack_kernel(len_ref, own_ref, wide_ref, *refs):
    (*narrow_refs, out_ref, start_ref, sel_ref) = refs

    @pl.when(pl.program_id(0) == 0)
    def _():
        select_rows(len_ref, own_ref, start_ref, sel_ref)

    sel = low(sel_ref[...])

    def pick(ref):
        return dot(sel, ref[...]).reshape(GROUPS, UNITS, ref.shape[1])

    wide = pick(wide_ref)
    narrow = [pick(ref) for ref in narrow_refs]
    for i in range(PACK_STEP):
        begin = i * RATIO * HD
        first, second = wide[:, :, begin : begin + PAIR], wide[:, :, begin + PAIR : begin + 2 * PAIR]
        parts = [(0, low(jnp.concatenate([first, second], axis=1)))]
        if narrow:
            both = low(jnp.concatenate([n[:, :, i * HD : (i + 1) * HD] for n in narrow], axis=1))
            parts.append((PAIR, both))
        for lane, both in parts:
            lanes = slice(lane, lane + both.shape[2])
            both = both.reshape(4, 2, 2, 16, both.shape[2])
            for h in range(2):
                for y in range(2):
                    out_ref[i // 2, h, 2 * (i % 2) + y, :, :, lanes] = both[:, h, y]


def pack(name, lengths, owner_docs, wide, *narrow):
    lanes = PAIR + (HD if narrow else 0)
    return pl.pallas_call(
        pack_kernel,
        grid=(KVH // PACK_STEP,),
        in_specs=[SMEM, SMEM, pl.BlockSpec((128, PACK_STEP * RATIO * HD), lambda i: (0, i))]
        + [pl.BlockSpec((128, PACK_STEP * HD), lambda i: (0, i)) for _ in narrow],
        out_specs=pl.BlockSpec((PACK_STEP // 2, 2, 4, 4, 16, lanes), lambda i: (i, 0, 0, 0, 0, 0)),
        out_shape=shape((4, 2, 4, 4, 16, lanes)),
        scratch_shapes=[pltpu.SMEM((2 * GROUPS,), jnp.int32), pltpu.VMEM((128, 128), jnp.float32)],
        compiler_params=pltpu.CompilerParams(vmem_limit_bytes=56 * MIB),
        name=name,
    )(lengths, owner_docs, wide, *narrow)


def fold(tile, how):
    return how(tile.reshape(tile.shape[0] // 8, 8, tile.shape[1]), axis=0)


def place(len_ref):
    group = lax.axis_index("x") * 4 + lax.axis_index("zh") * 2 + lax.axis_index("y") % 2
    return lax.axis_index("core"), len_ref[0, group]


def causal_bias(core):
    key = lax.broadcasted_iota(jnp.int32, (256, QROWS), 0)
    query = lax.broadcasted_iota(jnp.int32, (256, QROWS), 1)
    key_core = jnp.where(key < 128, core, 1 - core)
    key_pos = (key % 8) * 32 + key_core * 16 + (key // 8) % SPAN
    query_pos = (query % 8) * 32 + core * 16 + (query // 8) % SPAN
    return jnp.where(key_pos <= query_pos, 0.0, -1e30)


def sort_rows(order, ref, part):
    y = 2 * (part % 2)
    rows = ref[part // 2, :, y : y + 2]
    return low(dot(order, rows.reshape(256, rows.shape[4])))


def place_heads(placed, part, ref):
    for h in range(RATIO):
        here = slice(h * 128 + part * 16, h * 128 + (part + 1) * 16)
        row, lane = (h // 2) * 128, (h % 2) * HD
        ref[:, here, :] = placed[row : row + 128, lane : lane + HD].reshape(UNITS, 16, HD)


def unit_rows(c):
    return pl.ds(pl.multiple_of(c * 8, 8), 8)


def forward_kernel(
    info_ref, x_ref, oth_ref, o_ref, q_ref, k_ref, v_ref, stat_ref, turned_ref, kt_ref, vt_ref, s_ref, bias_ref, ot_ref, wide_ref
):
    core, first_len = place(info_ref)
    order = take_order()
    bias_ref[...] = causal_bias(core)
    for part in range(SPAN // 2):
        own = sort_rows(order, x_ref, part)
        place_heads(own, part, q_ref)
        for base, placed in ((0, own[:, PAIR:]), (128, sort_rows(order, oth_ref, part))):
            here = slice(base + part * 16, base + (part + 1) * 16)
            k_ref[:, here, :] = placed[:128].reshape(UNITS, 16, HD)
            v_ref[:, here, :] = placed[128:].reshape(UNITS, 16, HD)
    eye_hd = eye(HD)
    for c in range(UNITS):
        vt_ref[c] = low(dot_nt(eye_hd, v_ref[c]))
        kt_ref[c] = low(dot_nt(eye_hd, k_ref[c]))

    def one_unit(base, r):
        c = base + r
        q4 = q_ref[c]

        def attend_units(units):
            peak = None
            for i, j in enumerate(units):
                tile = dot_nt(k_ref[j], q4)
                if i == len(units) - 1:
                    tile = tile + bias_ref[...]
                s_ref[i] = tile
                top = fold(tile, jnp.max)
                peak = top if peak is None else jnp.maximum(peak, top)
            peak = jnp.max(peak, axis=0, keepdims=True) * EXP2_SCALE
            norm = jnp.zeros((8, QROWS), jnp.float32)
            for i in range(len(units)):
                tile = jnp.exp2(s_ref[i] * EXP2_SCALE - peak)
                s_ref[i] = tile
                norm = norm + fold(tile, jnp.sum)
            norm = jnp.sum(norm, axis=0, keepdims=True)
            inverse = 1.0 / norm
            stat_ref[c, 0:1, :] = peak + jnp.log2(norm)
            ot_ref[...] = sum(dot(vt_ref[j], low(s_ref[i] * inverse)) for i, j in enumerate(units))

        own = [base + j for j in range(r + 1)]
        whole = jnp.logical_and(base > 0, first_len > UNITS // 2)
        pl.when(whole)(lambda: attend_units(list(range(UNITS // 2)) + own))
        pl.when(jnp.logical_not(whole))(lambda: attend_units(own))
        out_low = low(ot_ref[...])
        turned_ref[c] = out_low
        for h in range(RATIO):
            part = dot_nt(eye_hd, out_low[:, h * 128 : (h + 1) * 128])
            wide_ref[:, unit_rows(c), h * HD : (h + 1) * HD] = part.reshape(SPAN, 8, HD)

    def one_half(half, carry):
        for r in range(UNITS // 2):
            one_unit(half * (UNITS // 2), r)
        return carry

    lax.fori_loop(0, 2, one_half, 0)
    o_ref[...] = low(wide_ref[...])


def forward(info, arrived, kv_oth):
    return pl.pallas_call(
        forward_kernel,
        in_specs=[SMEM, VMEM, VMEM],
        out_specs=[VMEM] * 7,
        out_shape=[
            shape((SPAN, 64, RATIO * HD)),
            shape((UNITS, QROWS, HD)),
            shape((UNITS, 256, HD)),
            shape((UNITS, 256, HD)),
            shape((UNITS, 8, QROWS), jnp.float32),
            shape((UNITS, HD, QROWS)),
            shape((UNITS, HD, 256)),
        ],
        scratch_shapes=[
            pltpu.VMEM((UNITS, HD, 256), jnp.bfloat16),
            pltpu.VMEM((UNITS, 256, QROWS), jnp.float32),
            pltpu.VMEM((256, QROWS), jnp.float32),
            pltpu.VMEM((HD, QROWS), jnp.float32),
            pltpu.VMEM((SPAN, 64, RATIO * HD), jnp.float32),
        ],
        compiler_params=pltpu.CompilerParams(vmem_limit_bytes=60 * MIB),
        cost_estimate=pl.CostEstimate(
            flops=5_000_000_000, bytes_accessed=8_000_000, transcendentals=5_000_000
        ),
        name="attend_forward",
    )(info, arrived, kv_oth)


def backward_kernel(
    info_ref, x_ref, q_ref, k_ref, v_ref, stat_ref, turned_ref, kt_ref, grad_ref, oth_ref, g_ref, bias_ref, dk_ref, dv_ref, dqt_ref, delta_ref
):
    core, first_len = place(info_ref)
    order = take_order()
    bias_ref[...] = causal_bias(core)
    for part in range(SPAN // 2):
        place_heads(sort_rows(order, x_ref, part), part, g_ref)
    eye_hd = eye(HD)
    for c in range(UNITS):
        product = turned_ref[c].astype(jnp.float32) * dot_nt(eye_hd, g_ref[c])
        delta_ref[c, 0:1, :] = jnp.sum(product, axis=0, keepdims=True)
    dk_ref[...] = jnp.zeros_like(dk_ref)
    dv_ref[...] = jnp.zeros_like(dv_ref)

    def one_unit(base, r):
        c = base + r
        q4, g4 = q_ref[c], g_ref[c]
        delta = delta_ref[c, 0:1, :]
        level = stat_ref[c, 0:1, :]

        def tiles(units, diagonal):
            scores = [dot_nt(k_ref[j], q4) for j in units]
            if diagonal:
                scores[-1] = scores[-1] + bias_ref[...]
            probs = [jnp.exp2(tile * EXP2_SCALE - level) for tile in scores]
            dprobs = [dot_nt(v_ref[j], g4) for j in units]
            dscores = [low(p * (d - delta)) for p, d in zip(probs, dprobs)]
            for j, p, d in zip(units, probs, dscores):
                dv_ref[j] += dot(low(p), g4)
                dk_ref[j] += dot(d, q4)
            return sum(dot(kt_ref[j], d) for j, d in zip(units, dscores))

        own = [base + j for j in range(r + 1)]
        whole = jnp.logical_and(base > 0, first_len > UNITS // 2)

        def attend_units(units):
            pairs = [units[max(0, end - 2) : end] for end in range(len(units), 0, -2)]
            dqt_ref[c] = sum(tiles(pair, i == 0) for i, pair in enumerate(pairs))

        pl.when(whole)(lambda: attend_units(list(range(UNITS // 2)) + own))
        pl.when(jnp.logical_not(whole))(lambda: attend_units(own))

    def one_half(half, carry):
        for r in range(UNITS // 2):
            one_unit(half * (UNITS // 2), r)
        return carry

    lax.fori_loop(0, 2, one_half, 0)
    for c in range(0, UNITS, 2):
        rows = slice(c * 8, (c + 2) * 8)
        for h in range(RATIO):
            pair = [low(dqt_ref[c + u, :, h * 128 : (h + 1) * 128] * SCALE) for u in range(2)]
            pair = [dot_nt(eye_hd, part).reshape(SPAN, 8, HD) for part in pair]
            grad_ref[:, rows, h * HD : (h + 1) * HD] = low(jnp.concatenate(pair, axis=1))
        for i, (ref, lane) in enumerate(((grad_ref, RATIO * HD), (oth_ref, 0))):
            keys = slice(i * 128, (i + 1) * 128)
            for half, (sums, scale) in enumerate(((dk_ref, SCALE), (dv_ref, 1.0))):
                pair = [(sums[c + u, keys] * scale).reshape(SPAN, 8, HD) for u in range(2)]
                begin = lane + half * HD
                ref[:, rows, begin : begin + HD] = low(jnp.concatenate(pair, axis=1))


def backward(info, grad, *saved):
    return pl.pallas_call(
        backward_kernel,
        in_specs=[SMEM] + [VMEM] * 7,
        out_specs=[VMEM] * 2,
        out_shape=[
            shape((SPAN, 64, 6 * HD)),
            shape((SPAN, 64, 2 * HD)),
        ],
        scratch_shapes=[
            pltpu.VMEM((UNITS, QROWS, HD), jnp.bfloat16),
            pltpu.VMEM((256, QROWS), jnp.float32),
            pltpu.VMEM((UNITS, 256, HD), jnp.float32),
            pltpu.VMEM((UNITS, 256, HD), jnp.float32),
            pltpu.VMEM((UNITS, HD, QROWS), jnp.float32),
            pltpu.VMEM((UNITS, 8, QROWS), jnp.float32),
        ],
        compiler_params=pltpu.CompilerParams(vmem_limit_bytes=60 * MIB),
        cost_estimate=pl.CostEstimate(
            flops=12_000_000_000, bytes_accessed=8_000_000, transcendentals=5_000_000
        ),
        name="attend_backward",
    )(info, grad, *saved)


def join_kernel(own_ref, oth_ref, out_ref):
    out_ref[...] = low(own_ref[...].astype(jnp.float32) + oth_ref[...].astype(jnp.float32))


def join(gradients, oth):
    step = SPAN // 2
    block = (step, 64, 2 * HD)
    return pl.pallas_call(
        join_kernel,
        grid=(2,),
        in_specs=[
            pl.BlockSpec(block, lambda i: (i, 0, 2)),
            pl.BlockSpec(block, lambda i: (i, 0, 0)),
        ],
        out_specs=pl.BlockSpec(block, lambda i: (i, 0, 2)),
        out_shape=shape((SPAN, 64, 6 * HD)),
        input_output_aliases={0: 0},
        compiler_params=pltpu.CompilerParams(vmem_limit_bytes=60 * MIB),
        name="join_gradients",
    )(gradients, oth)


def row_order(core):
    row = lax.broadcasted_iota(jnp.int32, (128, 128), 0)
    col = lax.broadcasted_iota(jnp.int32, (128, 128), 1)
    other = jnp.where(row % 2 == core, 0, 64)
    return low(jnp.where(col == other + (row // 16) * 8 + (row % 16) // 2, 1.0, 0.0))


def unpack_kernel(widths, z_ref, oth_ref, *out_refs):
    core = lax.axis_index("core")
    order = row_order(core)
    for g in range(KVH):
        both = jnp.concatenate([z_ref[g, core], oth_ref[g]], axis=0)
        placed = low(dot(order, both))
        begin = 0
        for width, ref in zip(widths, out_refs):
            ref[:, g * width : (g + 1) * width] = placed[:, begin : begin + width]
            begin += width


def unpack(z, oth, widths):
    return pl.pallas_call(
        functools.partial(unpack_kernel, widths),
        in_specs=[VMEM, VMEM],
        out_specs=[VMEM] * len(widths),
        out_shape=[shape((128, KVH * width)) for width in widths],
        compiler_params=pltpu.CompilerParams(vmem_limit_bytes=24 * MIB),
        name="unpack_rows",
    )(z, oth)


def body(queries, keys, values, out_grad, doc_lengths, owner_docs):
    core = lax.axis_index("core")
    lengths = doc_lengths.T

    def swap(tensor):
        return lax.ppermute(tensor, "core", [(0, 1), (1, 0)])

    def spread(tensor):
        return lax.all_to_all(tensor, ("zl", "y"), split_axis=0, concat_axis=0, tiled=True)

    def finish(tensor, widths):
        split = tensor.reshape((KVH, 2) + tensor.shape[1:])
        oth = swap(lax.dynamic_index_in_dim(split, 1 - core, 1, keepdims=False))
        return unpack(split, oth, widths)

    def gather(tensor):
        flat = tensor.reshape((BLOCKS * SPAN,) + tensor.shape[4:])
        moved = lax.all_to_all(flat, ("zl", "zh", "y", "x"), split_axis=0, concat_axis=0, tiled=True)
        return moved.reshape(tensor.shape)

    qkv = gather(pack("pack_qkv", lengths, owner_docs, queries, keys, values))
    packed_grad = pack("pack_grad", lengths, owner_docs, out_grad)
    qkv, packed_grad = lax.optimization_barrier((qkv, packed_grad))
    grad = gather(packed_grad)
    kv_oth = swap(qkv[..., PAIR:])
    out, *saved = forward(lengths, qkv, kv_oth)
    out, grad = lax.optimization_barrier((out, grad))
    out_back = spread(out)
    gradients, oth = backward(lengths, grad, *saved)
    gradients = join(gradients, swap(oth))
    gradients, out_back = lax.optimization_barrier((gradients, out_back))
    back = spread(gradients)
    (attn_out,) = finish(out_back, (RATIO * HD,))
    back, attn_out = lax.optimization_barrier((back, attn_out))
    return (attn_out, *finish(back, (RATIO * HD, HD, HD)))


def solution(mesh):
    cut = Mesh(mesh.devices.reshape(4, 2, 2, 4, 4), ("x", "zh", "core", "zl", "y"))
    rows = P(("x", "zh", "core", "zl", "y"), None)
    return jax.shard_map(
        body,
        mesh=cut,
        in_specs=(rows, rows, rows, rows, P(), P()),
        out_specs=(rows, rows, rows, rows),
        check_vma=False,
    )
```

```python
import functools
import math

import jax
import jax.numpy as jnp
from jax import lax
from jax.experimental import pallas as pl
from jax.experimental.pallas import tpu as pltpu
from jax.sharding import Mesh
from jax.sharding import PartitionSpec as P

QH = 32
KVH = 8
HD = 128
GROUPS = 16
UNITS = 8
BLOCKS = 8
SPAN = 16
RATIO = QH // KVH
QROWS = RATIO * 128
PAIR = 2 * HD
LANES = PAIR + HD
PACK_STEP = 4
SCALE = 1.0 / math.sqrt(HD)
EXP2_SCALE = SCALE * math.log2(math.e)
NT = (((1,), (1,)), ((), ()))
MIB = 1024 * 1024
SMEM = pl.BlockSpec(memory_space=pltpu.SMEM)
VMEM = pl.BlockSpec(memory_space=pltpu.VMEM)


def shape(dims, kind=jnp.bfloat16):
    return jax.ShapeDtypeStruct(dims, kind)


def dot(left, right):
    return jnp.dot(left, right, preferred_element_type=jnp.float32)


def dot_nt(left, right):
    return lax.dot_general(left, right, NT, preferred_element_type=jnp.float32)


def low(value):
    return value.astype(jnp.bfloat16)


def eye(size):
    row = lax.broadcasted_iota(jnp.int32, (size, size), 0)
    col = lax.broadcasted_iota(jnp.int32, (size, size), 1)
    return low(jnp.where(row == col, 1.0, 0.0))


def take_order():
    row = lax.broadcasted_iota(jnp.int32, (256, 256), 0)
    col = lax.broadcasted_iota(jnp.int32, (256, 256), 1)
    wanted = (row % 2) * 128 + (row // 8 % 2) * 64 + (row // 2 % 4) * 16 + (row // 128) * 8
    wanted = wanted + (row // 16) % 8
    return low(jnp.where(col == wanted, 1.0, 0.0))


def select_rows(len_ref, own_ref, start_ref, sel_ref):
    docs = [own_ref[entry] for entry in range(2 * GROUPS)]
    sizes = [len_ref[doc & 1, doc >> 1] for doc in docs]
    total = jnp.int32(0)
    for doc, size in zip(docs, sizes):
        start_ref[doc] = total
        total = total + size
    unit = lax.broadcasted_iota(jnp.int32, (UNITS, 128), 0)
    column = lax.broadcasted_iota(jnp.int32, (UNITS, 128), 1)
    for b in range(GROUPS):
        first = len_ref[0, b]
        source = jnp.where(
            unit < first, start_ref[2 * b] + unit, start_ref[2 * b + 1] + unit - first
        )
        sel_ref[b * UNITS : (b + 1) * UNITS, :] = jnp.where(column == source, 1.0, 0.0)


def pack_kernel(len_ref, own_ref, wide_ref, *refs):
    (*narrow_refs, out_ref, start_ref, sel_ref) = refs

    @pl.when(pl.program_id(0) == 0)
    def _():
        select_rows(len_ref, own_ref, start_ref, sel_ref)

    sel = low(sel_ref[...])

    def pick(ref):
        return dot(sel, ref[...]).reshape(GROUPS, UNITS, ref.shape[1])

    wide = pick(wide_ref)
    narrow = [pick(ref) for ref in narrow_refs]
    for i in range(PACK_STEP):
        begin = i * RATIO * HD
        first, second = wide[:, :, begin : begin + PAIR], wide[:, :, begin + PAIR : begin + 2 * PAIR]
        parts = [(0, low(jnp.concatenate([first, second], axis=1)))]
        if narrow:
            both = low(jnp.concatenate([n[:, :, i * HD : (i + 1) * HD] for n in narrow], axis=1))
            parts.append((PAIR, both))
        for lane, both in parts:
            lanes = slice(lane, lane + both.shape[2])
            both = both.reshape(4, 2, 2, 16, both.shape[2])
            for h in range(2):
                for y in range(2):
                    out_ref[i // 2, h, 2 * (i % 2) + y, :, :, lanes] = both[:, h, y]


def pack(name, lengths, owner_docs, wide, *narrow):
    lanes = PAIR + (HD if narrow else 0)
    return pl.pallas_call(
        pack_kernel,
        grid=(KVH // PACK_STEP,),
        in_specs=[SMEM, SMEM, pl.BlockSpec((128, PACK_STEP * RATIO * HD), lambda i: (0, i))]
        + [pl.BlockSpec((128, PACK_STEP * HD), lambda i: (0, i)) for _ in narrow],
        out_specs=pl.BlockSpec((PACK_STEP // 2, 2, 4, 4, 16, lanes), lambda i: (i, 0, 0, 0, 0, 0)),
        out_shape=shape((4, 2, 4, 4, 16, lanes)),
        scratch_shapes=[pltpu.SMEM((2 * GROUPS,), jnp.int32), pltpu.VMEM((128, 128), jnp.float32)],
        compiler_params=pltpu.CompilerParams(vmem_limit_bytes=56 * MIB),
        name=name,
    )(lengths, owner_docs, wide, *narrow)


def fold(tile, how):
    return how(tile.reshape(tile.shape[0] // 8, 8, tile.shape[1]), axis=0)


def place(len_ref):
    group = lax.axis_index("x") * 4 + lax.axis_index("zh") * 2 + lax.axis_index("y") % 2
    return lax.axis_index("core"), len_ref[0, group]


def causal_bias(core):
    key = lax.broadcasted_iota(jnp.int32, (256, QROWS), 0)
    query = lax.broadcasted_iota(jnp.int32, (256, QROWS), 1)
    key_core = jnp.where(key < 128, core, 1 - core)
    key_pos = (key % 8) * 32 + key_core * 16 + (key // 8) % SPAN
    query_pos = (query % 8) * 32 + core * 16 + (query // 8) % SPAN
    return jnp.where(key_pos <= query_pos, 0.0, -1e30)


def sort_rows(order, ref, part):
    y = 2 * (part % 2)
    rows = ref[part // 2, :, y : y + 2]
    return low(dot(order, rows.reshape(256, rows.shape[4])))


def place_heads(placed, part, ref):
    for h in range(RATIO):
        here = slice(h * 128 + part * 16, h * 128 + (part + 1) * 16)
        row, lane = (h // 2) * 128, (h % 2) * HD
        ref[:, here, :] = placed[row : row + 128, lane : lane + HD].reshape(UNITS, 16, HD)


def unit_rows(c):
    return pl.ds(pl.multiple_of(c * 8, 8), 8)


def forward_kernel(
    info_ref, x_ref, oth_ref, o_ref, q_ref, k_ref, v_ref, stat_ref, turned_ref, kt_ref, vt_ref, s_ref, bias_ref, ot_ref, wide_ref
):
    core, first_len = place(info_ref)
    order = take_order()
    bias_ref[...] = causal_bias(core)
    for part in range(SPAN // 2):
        own = sort_rows(order, x_ref, part)
        place_heads(own, part, q_ref)
        for base, placed in ((0, own[:, PAIR:]), (128, sort_rows(order, oth_ref, part))):
            here = slice(base + part * 16, base + (part + 1) * 16)
            k_ref[:, here, :] = placed[:128].reshape(UNITS, 16, HD)
            v_ref[:, here, :] = placed[128:].reshape(UNITS, 16, HD)
    eye_hd = eye(HD)
    for c in range(UNITS):
        vt_ref[c] = low(dot_nt(eye_hd, v_ref[c]))
        kt_ref[c] = low(dot_nt(eye_hd, k_ref[c]))

    def one_unit(base, r):
        c = base + r
        q4 = q_ref[c]

        def attend_units(units):
            peak = None
            for i, j in enumerate(units):
                tile = dot_nt(k_ref[j], q4)
                if i == len(units) - 1:
                    tile = tile + bias_ref[...]
                s_ref[i] = tile
                top = fold(tile, jnp.max)
                peak = top if peak is None else jnp.maximum(peak, top)
            peak = jnp.max(peak, axis=0, keepdims=True) * EXP2_SCALE
            norm = jnp.zeros((8, QROWS), jnp.float32)
            for i in range(len(units)):
                tile = jnp.exp2(s_ref[i] * EXP2_SCALE - peak)
                s_ref[i] = tile
                norm = norm + fold(tile, jnp.sum)
            norm = jnp.sum(norm, axis=0, keepdims=True)
            inverse = 1.0 / norm
            stat_ref[c, 0:1, :] = peak + jnp.log2(norm)
            ot_ref[...] = sum(dot(vt_ref[j], low(s_ref[i] * inverse)) for i, j in enumerate(units))

        own = [base + j for j in range(r + 1)]
        whole = jnp.logical_and(base > 0, first_len > UNITS // 2)
        pl.when(whole)(lambda: attend_units(list(range(UNITS // 2)) + own))
        pl.when(jnp.logical_not(whole))(lambda: attend_units(own))
        out_low = low(ot_ref[...])
        turned_ref[c] = out_low
        for h in range(RATIO):
            part = dot_nt(eye_hd, out_low[:, h * 128 : (h + 1) * 128])
            wide_ref[:, unit_rows(c), h * HD : (h + 1) * HD] = part.reshape(SPAN, 8, HD)

    def one_half(half, carry):
        for r in range(UNITS // 2):
            one_unit(half * (UNITS // 2), r)
        return carry

    lax.fori_loop(0, 2, one_half, 0)
    o_ref[...] = low(wide_ref[...])


def forward(info, arrived, kv_oth):
    return pl.pallas_call(
        forward_kernel,
        in_specs=[SMEM, VMEM, VMEM],
        out_specs=[VMEM] * 7,
        out_shape=[
            shape((SPAN, 64, RATIO * HD)),
            shape((UNITS, QROWS, HD)),
            shape((UNITS, 256, HD)),
            shape((UNITS, 256, HD)),
            shape((UNITS, 8, QROWS), jnp.float32),
            shape((UNITS, HD, QROWS)),
            shape((UNITS, HD, 256)),
        ],
        scratch_shapes=[
            pltpu.VMEM((UNITS, HD, 256), jnp.bfloat16),
            pltpu.VMEM((UNITS, 256, QROWS), jnp.float32),
            pltpu.VMEM((256, QROWS), jnp.float32),
            pltpu.VMEM((HD, QROWS), jnp.float32),
            pltpu.VMEM((SPAN, 64, RATIO * HD), jnp.float32),
        ],
        compiler_params=pltpu.CompilerParams(vmem_limit_bytes=60 * MIB),
        cost_estimate=pl.CostEstimate(
            flops=5_000_000_000, bytes_accessed=8_000_000, transcendentals=5_000_000
        ),
        name="attend_forward",
    )(info, arrived, kv_oth)


def backward_kernel(
    info_ref, x_ref, q_ref, k_ref, v_ref, stat_ref, turned_ref, kt_ref, grad_ref, oth_ref, g_ref, bias_ref, dk_ref, dv_ref, dqt_ref, delta_ref
):
    core, first_len = place(info_ref)
    order = take_order()
    bias_ref[...] = causal_bias(core)
    for part in range(SPAN // 2):
        place_heads(sort_rows(order, x_ref, part), part, g_ref)
    eye_hd = eye(HD)
    for c in range(UNITS):
        product = turned_ref[c].astype(jnp.float32) * dot_nt(eye_hd, g_ref[c])
        delta_ref[c, 0:1, :] = jnp.sum(product, axis=0, keepdims=True)
    dk_ref[...] = jnp.zeros_like(dk_ref)
    dv_ref[...] = jnp.zeros_like(dv_ref)

    def one_unit(base, r):
        c = base + r
        q4, g4 = q_ref[c], g_ref[c]
        delta = delta_ref[c, 0:1, :]
        level = stat_ref[c, 0:1, :]

        def tiles(units, diagonal):
            scores = [dot_nt(k_ref[j], q4) for j in units]
            if diagonal:
                scores[-1] = scores[-1] + bias_ref[...]
            probs = [jnp.exp2(tile * EXP2_SCALE - level) for tile in scores]
            dprobs = [dot_nt(v_ref[j], g4) for j in units]
            dscores = [low(p * (d - delta)) for p, d in zip(probs, dprobs)]
            for j, p, d in zip(units, probs, dscores):
                dv_ref[j] += dot(low(p), g4)
                dk_ref[j] += dot(d, q4)
            return sum(dot(kt_ref[j], d) for j, d in zip(units, dscores))

        own = [base + j for j in range(r + 1)]
        whole = jnp.logical_and(base > 0, first_len > UNITS // 2)

        def attend_units(units):
            pairs = [units[max(0, end - 2) : end] for end in range(len(units), 0, -2)]
            dqt_ref[c] = sum(tiles(pair, i == 0) for i, pair in enumerate(pairs))

        pl.when(whole)(lambda: attend_units(list(range(UNITS // 2)) + own))
        pl.when(jnp.logical_not(whole))(lambda: attend_units(own))

    def one_half(half, carry):
        for r in range(UNITS // 2):
            one_unit(half * (UNITS // 2), r)
        return carry

    lax.fori_loop(0, 2, one_half, 0)
    for c in range(0, UNITS, 2):
        rows = slice(c * 8, (c + 2) * 8)
        for h in range(RATIO):
            pair = [low(dqt_ref[c + u, :, h * 128 : (h + 1) * 128] * SCALE) for u in range(2)]
            pair = [dot_nt(eye_hd, part).reshape(SPAN, 8, HD) for part in pair]
            grad_ref[:, rows, h * HD : (h + 1) * HD] = low(jnp.concatenate(pair, axis=1))
        for i, (ref, lane) in enumerate(((grad_ref, RATIO * HD), (oth_ref, 0))):
            keys = slice(i * 128, (i + 1) * 128)
            for half, (sums, scale) in enumerate(((dk_ref, SCALE), (dv_ref, 1.0))):
                pair = [(sums[c + u, keys] * scale).reshape(SPAN, 8, HD) for u in range(2)]
                begin = lane + half * HD
                ref[:, rows, begin : begin + HD] = low(jnp.concatenate(pair, axis=1))


def backward(info, grad, *saved):
    return pl.pallas_call(
        backward_kernel,
        in_specs=[SMEM] + [VMEM] * 7,
        out_specs=[VMEM] * 2,
        out_shape=[
            shape((SPAN, 64, 6 * HD)),
            shape((SPAN, 64, 2 * HD)),
        ],
        scratch_shapes=[
            pltpu.VMEM((UNITS, QROWS, HD), jnp.bfloat16),
            pltpu.VMEM((256, QROWS), jnp.float32),
            pltpu.VMEM((UNITS, 256, HD), jnp.float32),
            pltpu.VMEM((UNITS, 256, HD), jnp.float32),
            pltpu.VMEM((UNITS, HD, QROWS), jnp.float32),
            pltpu.VMEM((UNITS, 8, QROWS), jnp.float32),
        ],
        compiler_params=pltpu.CompilerParams(vmem_limit_bytes=60 * MIB),
        cost_estimate=pl.CostEstimate(
            flops=12_000_000_000, bytes_accessed=8_000_000, transcendentals=5_000_000
        ),
        name="attend_backward",
    )(info, grad, *saved)


def join(gradients, oth):
    begin = RATIO * HD
    own = lax.slice_in_dim(gradients, begin, 6 * HD, axis=2)
    total = low(own.astype(jnp.float32) + oth.astype(jnp.float32))
    return lax.dynamic_update_slice(gradients, total, (0, 0, begin))


def row_order(core):
    row = lax.broadcasted_iota(jnp.int32, (128, 128), 0)
    col = lax.broadcasted_iota(jnp.int32, (128, 128), 1)
    other = jnp.where(row % 2 == core, 0, 64)
    return low(jnp.where(col == other + (row // 16) * 8 + (row % 16) // 2, 1.0, 0.0))


def unpack_kernel(widths, z_ref, oth_ref, *out_refs):
    core = lax.axis_index("core")
    order = row_order(core)
    for g in range(KVH):
        both = jnp.concatenate([z_ref[g, core], oth_ref[g]], axis=0)
        placed = low(dot(order, both))
        begin = 0
        for width, ref in zip(widths, out_refs):
            ref[:, g * width : (g + 1) * width] = placed[:, begin : begin + width]
            begin += width


def unpack(z, oth, widths):
    return pl.pallas_call(
        functools.partial(unpack_kernel, widths),
        in_specs=[VMEM, VMEM],
        out_specs=[VMEM] * len(widths),
        out_shape=[shape((128, KVH * width)) for width in widths],
        compiler_params=pltpu.CompilerParams(vmem_limit_bytes=24 * MIB),
        name="unpack_rows",
    )(z, oth)


def body(queries, keys, values, out_grad, doc_lengths, owner_docs):
    core = lax.axis_index("core")
    lengths = doc_lengths.T

    def swap(tensor):
        return lax.ppermute(tensor, "core", [(0, 1), (1, 0)])

    def spread(tensor):
        return lax.all_to_all(tensor, ("zl", "y"), split_axis=0, concat_axis=0, tiled=True)

    def finish(tensor, widths):
        split = tensor.reshape((KVH, 2) + tensor.shape[1:])
        oth = swap(lax.dynamic_index_in_dim(split, 1 - core, 1, keepdims=False))
        return unpack(split, oth, widths)

    def gather(tensor):
        flat = tensor.reshape((BLOCKS * SPAN,) + tensor.shape[4:])
        moved = lax.all_to_all(flat, ("zl", "zh", "y", "x"), split_axis=0, concat_axis=0, tiled=True)
        return moved.reshape(tensor.shape)

    qkv = gather(pack("pack_qkv", lengths, owner_docs, queries, keys, values))
    packed_grad = pack("pack_grad", lengths, owner_docs, out_grad)
    qkv, packed_grad = lax.optimization_barrier((qkv, packed_grad))
    grad = gather(packed_grad)
    kv_oth = swap(qkv[..., PAIR:])
    out, *saved = forward(lengths, qkv, kv_oth)
    out, grad = lax.optimization_barrier((out, grad))
    out_back = spread(out)
    gradients, oth = backward(lengths, grad, *saved)
    gradients = join(gradients, swap(oth))
    gradients, out_back = lax.optimization_barrier((gradients, out_back))
    back = spread(gradients)
    (attn_out,) = finish(out_back, (RATIO * HD,))
    back, attn_out = lax.optimization_barrier((back, attn_out))
    return (attn_out, *finish(back, (RATIO * HD, HD, HD)))


def solution(mesh):
    cut = Mesh(mesh.devices.reshape(4, 2, 2, 4, 4), ("x", "zh", "core", "zl", "y"))
    rows = P(("x", "zh", "core", "zl", "y"), None)
    return jax.shard_map(
        body,
        mesh=cut,
        in_specs=(rows, rows, rows, rows, P(), P()),
        out_specs=(rows, rows, rows, rows),
        check_vma=False,
    )
```

```python
import functools
import math

import jax
import jax.numpy as jnp
from jax import lax
from jax.experimental import pallas as pl
from jax.experimental.pallas import tpu as pltpu
from jax.sharding import Mesh
from jax.sharding import PartitionSpec as P

QH = 32
KVH = 8
HD = 128
GROUPS = 16
UNITS = 8
BLOCKS = 8
SPAN = 16
RATIO = QH // KVH
QROWS = RATIO * 128
PAIR = 2 * HD
LANES = PAIR + HD
PACK_STEP = 4
SCALE = 1.0 / math.sqrt(HD)
EXP2_SCALE = SCALE * math.log2(math.e)
NT = (((1,), (1,)), ((), ()))
MIB = 1024 * 1024
SMEM = pl.BlockSpec(memory_space=pltpu.SMEM)
VMEM = pl.BlockSpec(memory_space=pltpu.VMEM)


def shape(dims, kind=jnp.bfloat16):
    return jax.ShapeDtypeStruct(dims, kind)


def dot(left, right):
    return jnp.dot(left, right, preferred_element_type=jnp.float32)


def dot_nt(left, right):
    return lax.dot_general(left, right, NT, preferred_element_type=jnp.float32)


def low(value):
    return value.astype(jnp.bfloat16)


def eye(size):
    row = lax.broadcasted_iota(jnp.int32, (size, size), 0)
    col = lax.broadcasted_iota(jnp.int32, (size, size), 1)
    return low(jnp.where(row == col, 1.0, 0.0))


def take_order():
    row = lax.broadcasted_iota(jnp.int32, (256, 256), 0)
    col = lax.broadcasted_iota(jnp.int32, (256, 256), 1)
    wanted = (row % 2) * 128 + (row // 8 % 2) * 64 + (row // 2 % 4) * 16 + (row // 128) * 8
    wanted = wanted + (row // 16) % 8
    return low(jnp.where(col == wanted, 1.0, 0.0))


def select_rows(len_ref, own_ref, start_ref, sel_ref):
    docs = [own_ref[entry] for entry in range(2 * GROUPS)]
    sizes = [len_ref[doc & 1, doc >> 1] for doc in docs]
    total = jnp.int32(0)
    for doc, size in zip(docs, sizes):
        start_ref[doc] = total
        total = total + size
    unit = lax.broadcasted_iota(jnp.int32, (UNITS, 128), 0)
    column = lax.broadcasted_iota(jnp.int32, (UNITS, 128), 1)
    for b in range(GROUPS):
        first = len_ref[0, b]
        source = jnp.where(
            unit < first, start_ref[2 * b] + unit, start_ref[2 * b + 1] + unit - first
        )
        sel_ref[b * UNITS : (b + 1) * UNITS, :] = jnp.where(column == source, 1.0, 0.0)


def pack_kernel(len_ref, own_ref, wide_ref, *refs):
    (*narrow_refs, out_ref, start_ref, sel_ref) = refs

    @pl.when(pl.program_id(0) == 0)
    def _():
        select_rows(len_ref, own_ref, start_ref, sel_ref)

    sel = low(sel_ref[...])

    def pick(ref):
        return dot(sel, ref[...]).reshape(GROUPS, UNITS, ref.shape[1])

    wide = pick(wide_ref)
    narrow = [pick(ref) for ref in narrow_refs]
    for i in range(PACK_STEP):
        begin = i * RATIO * HD
        first, second = wide[:, :, begin : begin + PAIR], wide[:, :, begin + PAIR : begin + 2 * PAIR]
        parts = [(0, low(jnp.concatenate([first, second], axis=1)))]
        if narrow:
            both = low(jnp.concatenate([n[:, :, i * HD : (i + 1) * HD] for n in narrow], axis=1))
            parts.append((PAIR, both))
        for lane, both in parts:
            lanes = slice(lane, lane + both.shape[2])
            both = both.reshape(4, 2, 2, 16, both.shape[2])
            for h in range(2):
                for y in range(2):
                    out_ref[i // 2, h, 2 * (i % 2) + y, :, :, lanes] = both[:, h, y]


def pack(name, lengths, owner_docs, wide, *narrow):
    lanes = PAIR + (HD if narrow else 0)
    return pl.pallas_call(
        pack_kernel,
        grid=(KVH // PACK_STEP,),
        in_specs=[SMEM, SMEM, pl.BlockSpec((128, PACK_STEP * RATIO * HD), lambda i: (0, i))]
        + [pl.BlockSpec((128, PACK_STEP * HD), lambda i: (0, i)) for _ in narrow],
        out_specs=pl.BlockSpec((PACK_STEP // 2, 2, 4, 4, 16, lanes), lambda i: (i, 0, 0, 0, 0, 0)),
        out_shape=shape((4, 2, 4, 4, 16, lanes)),
        scratch_shapes=[pltpu.SMEM((2 * GROUPS,), jnp.int32), pltpu.VMEM((128, 128), jnp.float32)],
        compiler_params=pltpu.CompilerParams(vmem_limit_bytes=56 * MIB),
        name=name,
    )(lengths, owner_docs, wide, *narrow)


def fold(tile, how):
    return how(tile.reshape(tile.shape[0] // 8, 8, tile.shape[1]), axis=0)


def place(len_ref):
    group = lax.axis_index("x") * 4 + lax.axis_index("zh") * 2 + lax.axis_index("y") % 2
    return lax.axis_index("core"), len_ref[0, group]


def causal_bias(core):
    key = lax.broadcasted_iota(jnp.int32, (256, QROWS), 0)
    query = lax.broadcasted_iota(jnp.int32, (256, QROWS), 1)
    key_core = jnp.where(key < 128, core, 1 - core)
    key_pos = (key % 8) * 32 + key_core * 16 + (key // 8) % SPAN
    query_pos = (query % 8) * 32 + core * 16 + (query // 8) % SPAN
    return jnp.where(key_pos <= query_pos, 0.0, -1e30)


def sort_rows(order, ref, part):
    y = 2 * (part % 2)
    rows = ref[part // 2, :, y : y + 2]
    return low(dot(order, rows.reshape(256, rows.shape[4])))


def place_heads(placed, part, ref):
    for h in range(RATIO):
        here = slice(h * 128 + part * 16, h * 128 + (part + 1) * 16)
        row, lane = (h // 2) * 128, (h % 2) * HD
        ref[:, here, :] = placed[row : row + 128, lane : lane + HD].reshape(UNITS, 16, HD)


def unit_rows(c):
    return pl.ds(pl.multiple_of(c * 8, 8), 8)


def forward_kernel(
    info_ref, x_ref, oth_ref, o_ref, q_ref, k_ref, v_ref, stat_ref, turned_ref, kt_ref, vt_ref, s_ref, bias_ref, ot_ref, wide_ref
):
    core, first_len = place(info_ref)
    order = take_order()
    bias_ref[...] = causal_bias(core)
    for part in range(SPAN // 2):
        own = sort_rows(order, x_ref, part)
        place_heads(own, part, q_ref)
        for base, placed in ((0, own[:, PAIR:]), (128, sort_rows(order, oth_ref, part))):
            here = slice(base + part * 16, base + (part + 1) * 16)
            k_ref[:, here, :] = placed[:128].reshape(UNITS, 16, HD)
            v_ref[:, here, :] = placed[128:].reshape(UNITS, 16, HD)
    eye_hd = eye(HD)
    for c in range(UNITS):
        vt_ref[c] = low(dot_nt(eye_hd, v_ref[c]))
        kt_ref[c] = low(dot_nt(eye_hd, k_ref[c]))

    def one_unit(base, r):
        c = base + r
        q4 = q_ref[c]

        def attend_units(units):
            peak = None
            for i, j in enumerate(units):
                tile = dot_nt(k_ref[j], q4)
                if i == len(units) - 1:
                    tile = tile + bias_ref[...]
                s_ref[i] = tile
                top = fold(tile, jnp.max)
                peak = top if peak is None else jnp.maximum(peak, top)
            peak = jnp.max(peak, axis=0, keepdims=True) * EXP2_SCALE
            norm = jnp.zeros((8, QROWS), jnp.float32)
            for i in range(len(units)):
                tile = jnp.exp2(s_ref[i] * EXP2_SCALE - peak)
                s_ref[i] = tile
                norm = norm + fold(tile, jnp.sum)
            norm = jnp.sum(norm, axis=0, keepdims=True)
            inverse = 1.0 / norm
            stat_ref[c, 0:1, :] = peak + jnp.log2(norm)
            ot_ref[...] = sum(dot(vt_ref[j], low(s_ref[i] * inverse)) for i, j in enumerate(units))

        own = [base + j for j in range(r + 1)]
        whole = jnp.logical_and(base > 0, first_len > UNITS // 2)
        pl.when(whole)(lambda: attend_units(list(range(UNITS // 2)) + own))
        pl.when(jnp.logical_not(whole))(lambda: attend_units(own))
        out_low = low(ot_ref[...])
        turned_ref[c] = out_low
        for h in range(RATIO):
            part = dot_nt(eye_hd, out_low[:, h * 128 : (h + 1) * 128])
            wide_ref[:, unit_rows(c), h * HD : (h + 1) * HD] = part.reshape(SPAN, 8, HD)

    def one_half(half, carry):
        for r in range(UNITS // 2):
            one_unit(half * (UNITS // 2), r)
        return carry

    lax.fori_loop(0, 2, one_half, 0)
    o_ref[...] = low(wide_ref[...])


def forward(info, arrived, kv_oth):
    return pl.pallas_call(
        forward_kernel,
        in_specs=[SMEM, VMEM, VMEM],
        out_specs=[VMEM] * 7,
        out_shape=[
            shape((SPAN, 64, RATIO * HD)),
            shape((UNITS, QROWS, HD)),
            shape((UNITS, 256, HD)),
            shape((UNITS, 256, HD)),
            shape((UNITS, 8, QROWS), jnp.float32),
            shape((UNITS, HD, QROWS)),
            shape((UNITS, HD, 256)),
        ],
        scratch_shapes=[
            pltpu.VMEM((UNITS, HD, 256), jnp.bfloat16),
            pltpu.VMEM((UNITS, 256, QROWS), jnp.float32),
            pltpu.VMEM((256, QROWS), jnp.float32),
            pltpu.VMEM((HD, QROWS), jnp.float32),
            pltpu.VMEM((SPAN, 64, RATIO * HD), jnp.float32),
        ],
        compiler_params=pltpu.CompilerParams(vmem_limit_bytes=60 * MIB),
        cost_estimate=pl.CostEstimate(
            flops=5_000_000_000, bytes_accessed=8_000_000, transcendentals=5_000_000
        ),
        name="attend_forward",
    )(info, arrived, kv_oth)


def backward_kernel(
    info_ref, x_ref, q_ref, k_ref, v_ref, stat_ref, turned_ref, kt_ref, grad_ref, oth_ref, g_ref, bias_ref, dk_ref, dv_ref, dqt_ref, delta_ref
):
    core, first_len = place(info_ref)
    order = take_order()
    bias_ref[...] = causal_bias(core)
    for part in range(SPAN // 2):
        place_heads(sort_rows(order, x_ref, part), part, g_ref)
    eye_hd = eye(HD)
    for c in range(UNITS):
        product = turned_ref[c].astype(jnp.float32) * dot_nt(eye_hd, g_ref[c])
        delta_ref[c, 0:1, :] = jnp.sum(product, axis=0, keepdims=True)

    def one_unit(base, r):
        c = base + r
        q4, g4 = q_ref[c], g_ref[c]
        delta = delta_ref[c, 0:1, :]
        level = stat_ref[c, 0:1, :]

        def tiles(units, diagonal):
            scores = [dot_nt(k_ref[j], q4) for j in units]
            if diagonal:
                scores[-1] = scores[-1] + bias_ref[...]
            probs = [jnp.exp2(tile * EXP2_SCALE - level) for tile in scores]
            dprobs = [dot_nt(v_ref[j], g4) for j in units]
            dscores = [low(p * (d - delta)) for p, d in zip(probs, dprobs)]
            for i, (j, p, d) in enumerate(zip(units, probs, dscores)):
                dv, dk = dot(low(p), g4), dot(d, q4)
                if diagonal and i == len(units) - 1:
                    dv_ref[j] = dv
                    dk_ref[j] = dk
                else:
                    dv_ref[j] += dv
                    dk_ref[j] += dk
            return sum(dot(kt_ref[j], d) for j, d in zip(units, dscores))

        own = [base + j for j in range(r + 1)]
        whole = jnp.logical_and(base > 0, first_len > UNITS // 2)

        def attend_units(units):
            pairs = [units[max(0, end - 2) : end] for end in range(len(units), 0, -2)]
            dqt_ref[c] = sum(tiles(pair, i == 0) for i, pair in enumerate(pairs))

        pl.when(whole)(lambda: attend_units(list(range(UNITS // 2)) + own))
        pl.when(jnp.logical_not(whole))(lambda: attend_units(own))

    def one_half(half, carry):
        for r in range(UNITS // 2):
            one_unit(half * (UNITS // 2), r)
        return carry

    lax.fori_loop(0, 2, one_half, 0)
    for c in range(0, UNITS, 2):
        rows = slice(c * 8, (c + 2) * 8)
        for h in range(RATIO):
            pair = [low(dqt_ref[c + u, :, h * 128 : (h + 1) * 128] * SCALE) for u in range(2)]
            pair = [dot_nt(eye_hd, part).reshape(SPAN, 8, HD) for part in pair]
            grad_ref[:, rows, h * HD : (h + 1) * HD] = low(jnp.concatenate(pair, axis=1))
        for i, (ref, lane) in enumerate(((grad_ref, RATIO * HD), (oth_ref, 0))):
            keys = slice(i * 128, (i + 1) * 128)
            for half, (sums, scale) in enumerate(((dk_ref, SCALE), (dv_ref, 1.0))):
                pair = [(sums[c + u, keys] * scale).reshape(SPAN, 8, HD) for u in range(2)]
                begin = lane + half * HD
                ref[:, rows, begin : begin + HD] = low(jnp.concatenate(pair, axis=1))


def backward(info, grad, *saved):
    return pl.pallas_call(
        backward_kernel,
        in_specs=[SMEM] + [VMEM] * 7,
        out_specs=[VMEM] * 2,
        out_shape=[
            shape((SPAN, 64, 6 * HD)),
            shape((SPAN, 64, 2 * HD)),
        ],
        scratch_shapes=[
            pltpu.VMEM((UNITS, QROWS, HD), jnp.bfloat16),
            pltpu.VMEM((256, QROWS), jnp.float32),
            pltpu.VMEM((UNITS, 256, HD), jnp.float32),
            pltpu.VMEM((UNITS, 256, HD), jnp.float32),
            pltpu.VMEM((UNITS, HD, QROWS), jnp.float32),
            pltpu.VMEM((UNITS, 8, QROWS), jnp.float32),
        ],
        compiler_params=pltpu.CompilerParams(vmem_limit_bytes=60 * MIB),
        cost_estimate=pl.CostEstimate(
            flops=12_000_000_000, bytes_accessed=8_000_000, transcendentals=5_000_000
        ),
        name="attend_backward",
    )(info, grad, *saved)


def join(gradients, oth):
    begin = RATIO * HD
    own = lax.slice_in_dim(gradients, begin, 6 * HD, axis=2)
    total = low(own.astype(jnp.float32) + oth.astype(jnp.float32))
    return lax.dynamic_update_slice(gradients, total, (0, 0, begin))


def row_order(core):
    row = lax.broadcasted_iota(jnp.int32, (128, 128), 0)
    col = lax.broadcasted_iota(jnp.int32, (128, 128), 1)
    other = jnp.where(row % 2 == core, 0, 64)
    return low(jnp.where(col == other + (row // 16) * 8 + (row % 16) // 2, 1.0, 0.0))


def unpack_kernel(widths, z_ref, oth_ref, *refs):
    count = len(widths)
    out_refs, staged, sems = refs[:count], refs[count : 2 * count], refs[2 * count]
    core = lax.axis_index("core")
    order = row_order(core)
    copies = []
    for g in range(KVH):
        both = jnp.concatenate([z_ref[g, core], oth_ref[g]], axis=0)
        placed = low(dot(order, both))
        begin = 0
        for i, width in enumerate(widths):
            staged[i][:, g * width : (g + 1) * width] = placed[:, begin : begin + width]
            begin += width
        if g % 2:
            for i, width in enumerate(widths):
                lanes = pl.ds((g - 1) * width, 2 * width)
                copy = pltpu.make_async_copy(
                    staged[i].at[:, lanes], out_refs[i].at[:, lanes], sems.at[i, g // 2]
                )
                copy.start()
                copies.append(copy)
    for copy in copies:
        copy.wait()


def unpack(z, oth, widths):
    return pl.pallas_call(
        functools.partial(unpack_kernel, widths),
        in_specs=[VMEM, VMEM],
        out_specs=[pl.BlockSpec(memory_space=pl.ANY)] * len(widths),
        out_shape=[shape((128, KVH * width)) for width in widths],
        scratch_shapes=[pltpu.VMEM((128, KVH * width), jnp.bfloat16) for width in widths]
        + [pltpu.SemaphoreType.DMA((len(widths), KVH // 2))],
        compiler_params=pltpu.CompilerParams(vmem_limit_bytes=24 * MIB),
        name="unpack_rows",
    )(z, oth)


def body(queries, keys, values, out_grad, doc_lengths, owner_docs):
    core = lax.axis_index("core")
    lengths = doc_lengths.T

    def swap(tensor):
        return lax.ppermute(tensor, "core", [(0, 1), (1, 0)])

    def spread(tensor):
        return lax.all_to_all(tensor, ("zl", "y"), split_axis=0, concat_axis=0, tiled=True)

    def finish(tensor, widths):
        split = tensor.reshape((KVH, 2) + tensor.shape[1:])
        oth = swap(lax.dynamic_index_in_dim(split, 1 - core, 1, keepdims=False))
        return unpack(split, oth, widths)

    def gather(tensor):
        flat = tensor.reshape((BLOCKS * SPAN,) + tensor.shape[4:])
        moved = lax.all_to_all(flat, ("zl", "zh", "y", "x"), split_axis=0, concat_axis=0, tiled=True)
        return moved.reshape(tensor.shape)

    qkv = gather(pack("pack_qkv", lengths, owner_docs, queries, keys, values))
    packed_grad = pack("pack_grad", lengths, owner_docs, out_grad)
    qkv, packed_grad = lax.optimization_barrier((qkv, packed_grad))
    grad = gather(packed_grad)
    kv_oth = swap(qkv[..., PAIR:])
    out, *saved = forward(lengths, qkv, kv_oth)
    out, grad = lax.optimization_barrier((out, grad))
    out_back = spread(out)
    gradients, oth = backward(lengths, grad, *saved)
    gradients = join(gradients, swap(oth))
    gradients, out_back = lax.optimization_barrier((gradients, out_back))
    back = spread(gradients)
    (attn_out,) = finish(out_back, (RATIO * HD,))
    back, attn_out = lax.optimization_barrier((back, attn_out))
    return (attn_out, *finish(back, (RATIO * HD, HD, HD)))


def solution(mesh):
    cut = Mesh(mesh.devices.reshape(4, 2, 2, 4, 4), ("x", "zh", "core", "zl", "y"))
    rows = P(("x", "zh", "core", "zl", "y"), None)
    return jax.shard_map(
        body,
        mesh=cut,
        in_specs=(rows, rows, rows, rows, P(), P()),
        out_specs=(rows, rows, rows, rows),
        check_vma=False,
    )
```
